256 devices in a mesh: group: 2 (over y_lo), rows: 128 (over y_hi, z, x, core).
Axes of the slice: x: 4, y: 4 (y_hi: 2, y_lo: 2; y = y_hi * 2 + y_lo), z: 8, core: 2. Of those that a mesh axis runs over, the one named last changes fastest.
Arguments:
- embeds: bfloat16 [2, 16384, 768], P('group', 'rows'), may hold values from -8 to 8
- weights: bfloat16 [2, 768, 768], P('group', 'rows'), may hold values from -0.3 to 1.3
- pair_index: int32 [16384], replicated, may hold values from 0 to 16383, as said below
- scale: float32 [1], replicated, may hold values from 12 to 28
Outputs:
- embed_grad: bfloat16 [2, 16384, 768], P('group', 'rows')
- weight_grad: float32 [2, 768, 768], P('group', 'rows')
The draws below stay inside these ranges and needn't reach their ends.
Inputs may be any that keep to these rules, and one draw needn't show every extreme that they name: `pair_index`: a permutation of the 16384 rows.
All inputs are finite; a program needn't handle non-finite values.
Results may differ from the reference program's by a relative error of at most 0.0062.
Values may be sent and summed in bfloat16 or wider, within the bound.
No kernel may reach another device: no remote copies, remote signals or barrier semaphores. Data moves between devices by JAX's collectives and lax.ppermute only.
A program may use at most 128 MiB of HBM per device.

```python
import math
import jax
import jax.numpy as jnp
from jax import lax

D = 768
SAMPLES = 16384


def paired(key):
    order = jax.random.permutation(jax.random.fold_in(key, 11), SAMPLES).astype(jnp.int32)
    groups = max(SAMPLES // 8, 1)
    member = jax.random.randint(jax.random.fold_in(key, 14), (SAMPLES,), 0, groups).astype(jnp.int32)
    centers = jnp.clip(jax.random.normal(jax.random.fold_in(key, 15), (groups, D), jnp.float32), -4.0, 4.0)
    single = jnp.clip(jax.random.normal(jax.random.fold_in(key, 12), (SAMPLES, D), jnp.float32), -4.0, 4.0)
    base = 0.95 * jnp.take(centers, member, axis=0) + 0.3 * single
    strength = jax.random.uniform(jax.random.fold_in(key, 13), (SAMPLES, 1), jnp.float32, 0.0, 3.0)
    return (order, base, strength)


def draw_pair_index(key, part):
    order, base, strength = paired(key)
    return order


def draw_embeds(key, part):
    order, base, strength = paired(key)
    key = jax.random.fold_in(key, 2)
    noise = jnp.clip(jax.random.normal(jax.random.fold_in(key, 21), (2, SAMPLES, D), jnp.float32), -4.0, 4.0)
    image = base + 0.5 * noise[0]
    matched = strength * base + noise[1]
    modal = jnp.zeros((SAMPLES, D), jnp.float32).at[order].set(matched)
    return jnp.clip(jnp.stack([image, modal]) / math.sqrt(D), -8.0, 8.0).astype(jnp.bfloat16)


def draw_weights(key, part):
    key = jax.random.fold_in(key, 3)
    common = jnp.clip(jax.random.normal(jax.random.fold_in(key, 31), (D, D), jnp.float32), -4.0, 4.0)
    single = jnp.clip(jax.random.normal(jax.random.fold_in(key, 32), (2, D, D), jnp.float32), -4.0, 4.0)
    full = jnp.eye(D, dtype=jnp.float32)[None] + (0.35 * common[None] + 0.25 * single) / math.sqrt(D)
    return jnp.clip(full, -0.3, 1.3).astype(jnp.bfloat16)


def setup_inputs(seed: int = 0) -> dict:
    key_of = jax.random.split(jax.random.key(seed), 5)
    return {
        "embeds": draw_embeds(jax.random.fold_in(key_of[4], 71), 0),
        "weights": draw_weights(jax.random.fold_in(key_of[4], 71), 0),
        "pair_index": draw_pair_index(jax.random.fold_in(key_of[4], 71), 0),
        "scale": jnp.clip(jax.random.uniform(key_of[3], (1,), jnp.float32, 12.0, 28.0), 12.0, 28.0),
    }


EPS = 1e-06

def project(inputs, weight):
    proj = jnp.dot(inputs, weight, preferred_element_type=jnp.float32)
    inv = lax.rsqrt(lax.optimization_barrier(jnp.sum(proj * proj, axis=1, keepdims=True)) + EPS)
    return (proj * inv, inv)

def blocks(array, size):
    return array.reshape((array.shape[0] // size, size) + array.shape[1:])

def side_lse(mine, other, factor):
    size = math.gcd(SAMPLES, 512)

    def one(part):
        scores = factor * jnp.dot(part, other.T, preferred_element_type=jnp.float32)
        return jnp.log(lax.optimization_barrier(jnp.sum(jnp.exp(scores), axis=1)))
    return lax.map(one, blocks(mine, size)).reshape(SAMPLES)

def side_grad(mine, other, own_lse, other_lse, partner, factor):
    size = math.gcd(SAMPLES, 512)

    def one(pieces):
        part, lse_part, index = pieces
        scores = factor * jnp.dot(part, other.T, preferred_element_type=jnp.float32)
        weight_row = (jnp.exp(scores - lse_part[:, None]) + jnp.exp(scores - other_lse[None, :])).astype(jnp.bfloat16)
        positive = jnp.take(other, index, axis=0).astype(jnp.float32)
        return factor * (jnp.dot(weight_row, other, preferred_element_type=jnp.float32) - 2.0 * positive)
    result = lax.map(one, (blocks(mine, size), blocks(own_lse, size), blocks(partner, size)))
    return result.reshape(SAMPLES, D)

def finish(d_unit, unit, inv, inputs, weight):
    d_proj = (inv * (d_unit - unit * lax.optimization_barrier(jnp.sum(d_unit * unit, axis=1, keepdims=True)))).astype(jnp.bfloat16)
    d_inputs = jnp.dot(d_proj, weight.T, preferred_element_type=jnp.float32).astype(jnp.bfloat16)
    d_weight = jnp.dot(inputs.T, d_proj, preferred_element_type=jnp.float32)
    return (d_inputs, d_weight)

def reference(embeds, weights, pair_index, scale):
    factor = scale[0]
    iota = jnp.arange(SAMPLES, dtype=jnp.int32)
    inverse = jnp.zeros((SAMPLES,), jnp.int32).at[pair_index].set(iota)
    unit_img, inv_img = project(embeds[0], weights[0])
    unit_mod, inv_mod = project(embeds[1], weights[1])
    low_img = unit_img.astype(jnp.bfloat16)
    low_mod = unit_mod.astype(jnp.bfloat16)
    lse_img = side_lse(low_img, low_mod, factor)
    lse_mod = side_lse(low_mod, low_img, factor)
    grad_img = side_grad(low_img, low_mod, lse_img, lse_mod, pair_index, factor)
    grad_mod = side_grad(low_mod, low_img, lse_mod, lse_img, inverse, factor)
    dx_img, dw_img = finish(grad_img, unit_img, inv_img, embeds[0], weights[0])
    dx_mod, dw_mod = finish(grad_mod, unit_mod, inv_mod, embeds[1], weights[1])
    return (jnp.stack([dx_img, dx_mod]), jnp.stack([dw_img, dw_mod]))
```

```python
import jax
import jax.numpy as jnp
from jax import lax
from jax.sharding import Mesh, PartitionSpec as P

EPS = 1e-06
AXES = ("yl", "yh", "z", "x", "c")
SIZES = {"yl": 2, "yh": 2, "z": 8, "x": 4, "c": 2}
ROWS = ("yh", "z", "x", "c")
PLANE = ("yl", "yh", "x")
F32 = jnp.float32
BF16 = jnp.bfloat16


def count(axes):
    total = 1
    for name in axes:
        total *= SIZES[name]
    return total


def mirror(value, axes, mask=1):
    return lax.ppermute(value, axes, [(i, i ^ mask) for i in range(count(axes))])


def gather(value, axes):
    copies = jnp.broadcast_to(value[None], (count(axes),) + value.shape)
    return lax.all_to_all(copies, axes, 0, 0)


def total(value, steps):
    for axes, mask in steps:
        value = value + mirror(value, axes, mask)
    return value


def gather_weights(shard):
    rows, width = shard.shape
    half = width // 2
    core = lax.axis_index("c")
    other = mirror(shard, ("c",))
    both = jnp.where(core == 0, jnp.stack([shard, other]), jnp.stack([other, shard]))
    both = both.reshape(2 * rows, width)
    part = lax.dynamic_slice_in_dim(both, core * half, half, 1)
    part = gather(part, ("yh", "x")).reshape(2, 4 * 2 * rows, half)
    part = gather(part, ("z",))
    part = jnp.swapaxes(part, 0, 1).reshape(width, half)
    other = mirror(part, ("c",))
    return jnp.where(
        core == 0,
        jnp.concatenate([part, other], 1),
        jnp.concatenate([other, part], 1),
    )


def scatter_weight_grad(partial):
    width = partial.shape[0]
    half = width // 2
    rows = width // 128
    core = lax.axis_index("c")
    mine = lax.dynamic_slice_in_dim(partial, core * half, half, 1)
    send = lax.dynamic_slice_in_dim(partial, (1 - core) * half, half, 1)
    part = mine + mirror(send, ("c",))
    part = part.astype(BF16).reshape(2, 8, 8 * rows, half)
    part = lax.all_to_all(jnp.swapaxes(part, 0, 1), ("z",), 0, 0)
    part = jnp.sum(part.astype(F32), axis=0).reshape(8, 2 * rows, half)
    part = jnp.sum(lax.all_to_all(part, ("yh", "x"), 0, 0), axis=0)
    part = part.reshape(2, rows, half)
    mine = lax.dynamic_index_in_dim(part, core, 0, False)
    other = mirror(lax.dynamic_index_in_dim(part, 1 - core, 0, False), ("c",))
    return jnp.where(
        core == 0,
        jnp.concatenate([mine, other], 1),
        jnp.concatenate([other, mine], 1),
    )


def per_device(embeds, weights, pair_index, scale):
    factor = scale[0]
    side = lax.axis_index("yl")
    yh, z, x, core = [lax.axis_index(name) for name in ROWS]
    own = embeds[0]
    here, width = own.shape
    half = here // 2
    weight = gather_weights(weights[0])
    proj = jnp.dot(own, weight, preferred_element_type=F32)
    inv = lax.rsqrt(jnp.sum(proj * proj, axis=1, keepdims=True) + EPS)
    unit = proj * inv
    low = unit.astype(BF16)

    keep = lax.dynamic_slice_in_dim(low, side * half, half, 0)
    send = lax.dynamic_slice_in_dim(low, (1 - side) * half, half, 0)
    came = mirror(send, ("yl",))
    image = jnp.where(side == 0, keep, came)
    modal = jnp.where(side == 0, came, keep)

    image = gather(image, PLANE).reshape(16 * half, width)
    modal = gather(modal, ("z",)).reshape(8 * half, width)
    other = mirror(modal, ("c",))
    modal = jnp.where(
        core == 0, jnp.concatenate([modal, other]), jnp.concatenate([other, modal])
    )

    table = pair_index.reshape(2, 8, 4, 2, 2, half)
    table = lax.dynamic_index_in_dim(table, z, 1, False)
    table = lax.dynamic_index_in_dim(table, core, 2, False)
    partner = table.transpose(2, 0, 1, 3).reshape(16 * half)
    cc, zz, rr = jnp.arange(2), jnp.arange(8), jnp.arange(half)
    ids = (((yh * 8 + zz[None, :, None]) * 4 + x) * 2 + cc[:, None, None]) * here
    ids = (ids + side * half + rr[None, None, :]).reshape(16 * half)

    scores = factor * lax.dot_general(
        image, modal, (((1,), (1,)), ((), ())), preferred_element_type=F32
    )
    power = jnp.exp(scores)
    row_sum = total(
        jnp.sum(power, axis=1), [(("x",), 1), (("x",), 3), (("yl", "yh"), 2), (("yl", "yh"), 3)]
    )
    col_sum = total(
        jnp.sum(power, axis=0), [(("c",), 1), (("z",), 1), (("z",), 2), (("z",), 4)]
    )
    hit = partner[:, None] == ids[None, :]
    weight_row = power * (1.0 / row_sum[:, None] + 1.0 / col_sum[None, :])
    weight_row = (weight_row - jnp.where(hit, 2.0, 0.0)).astype(BF16)

    d_modal = lax.dot_general(
        weight_row, image, (((0,), (0,)), ((), ())), preferred_element_type=F32
    )
    d_modal = d_modal.reshape(2, 8 * half, width)
    mine = lax.dynamic_index_in_dim(d_modal, core, 0, False)
    send = lax.dynamic_index_in_dim(d_modal, 1 - core, 0, False).astype(BF16)
    d_modal = (mine + mirror(send, ("c",)).astype(F32)).astype(BF16)
    d_modal = lax.all_to_all(d_modal.reshape(8, half, width), ("z",), 0, 0)
    d_modal = jnp.sum(d_modal.astype(F32), axis=0)

    d_image = jnp.dot(weight_row, modal, preferred_element_type=F32).astype(BF16)
    d_image = lax.all_to_all(d_image.reshape(16, half, width), PLANE, 0, 0)
    d_image = jnp.sum(d_image.astype(F32), axis=0)

    came = mirror(jnp.where(side == 0, d_modal, d_image), ("yl",))
    d_unit = jnp.where(
        side == 0,
        jnp.concatenate([d_image, came]),
        jnp.concatenate([came, d_modal]),
    )
    d_unit = factor * d_unit
    d_proj = inv * (d_unit - unit * jnp.sum(d_unit * unit, axis=1, keepdims=True))
    d_proj = d_proj.astype(BF16)
    d_inputs = lax.dot_general(
        d_proj, weight, (((1,), (1,)), ((), ())), preferred_element_type=F32
    )
    d_weight = lax.dot_general(
        own, d_proj, (((0,), (0,)), ((), ())), preferred_element_type=F32
    )
    return (d_inputs.astype(BF16)[None], scatter_weight_grad(d_weight)[None])


def solution(mesh):
    devices = mesh.devices.reshape([SIZES[name] for name in AXES])
    return jax.shard_map(
        per_device,
        mesh=Mesh(devices, AXES),
        in_specs=(P("yl", ROWS, None), P("yl", ROWS, None), P(), P()),
        out_specs=(P("yl", ROWS, None), P("yl", ROWS, None)),
        check_vma=False,
    )
```

```python
import jax
import jax.numpy as jnp
from jax import lax
from jax.experimental import pallas as pl
from jax.experimental.pallas import tpu as pltpu
from jax.sharding import Mesh, PartitionSpec as P

EPS = 1e-06
AXES = ("yl", "yh", "z", "x", "c")
SIZES = {"yl": 2, "yh": 2, "z": 8, "x": 4, "c": 2}
ROWS = ("yh", "z", "x", "c")
PLANE = ("yl", "yh", "x")
Y = ("yl", "yh")
F32 = jnp.float32
BF16 = jnp.bfloat16
LIMIT = 56 << 20
MEET = (0, 1, -1, -2, 2, 3, -3, -4)


def count(axes):
    total = 1
    for name in axes:
        total *= SIZES[name]
    return total


def mirror(value, axes, mask=1):
    return lax.ppermute(value, axes, [(i, i ^ mask) for i in range(count(axes))])


def pair(value, kind):
    size = SIZES["z"]
    return lax.ppermute(value, "z", [(i, (((i + kind) ^ 1) - kind) % size) for i in range(size)])


def meets(z, kind):
    sign = 1 - 2 * ((z + kind) & 1)
    return [(z + sign * step) & 7 for step in MEET]


def gather(value, axes):
    copies = jnp.broadcast_to(value[None], (count(axes),) + value.shape)
    return lax.all_to_all(copies, axes, 0, 0)


def stage(*values):
    return lax.optimization_barrier(values)


def wider(value):
    return value.astype(F32)


def column(row):
    return jnp.transpose(jnp.broadcast_to(row, (128, row.shape[1])))[:, :1]


def line(values):
    return jnp.transpose(jnp.broadcast_to(values, (values.shape[0], 128)))[:1]


def mover(sems):
    used = []

    def move(source, target):
        copy = pltpu.make_async_copy(source, target, sems.at[len(used)])
        used.append(copy)
        copy.start()
        return copy

    return move


def arrive(copies):
    for copy in copies:
        copy.wait()


def fill(tile, values, first):
    for k in range(values.shape[1] // 128):
        tile[first + k : first + k + 1, :] = values[:, k * 128 : (k + 1) * 128]


def spread(tile):
    return jnp.concatenate([tile[k : k + 1, :] for k in range(tile.shape[0])], axis=1)


def score_kernel(at, scale, h_img, *refs):
    met = [refs[i * 5 : i * 5 + 5] for i in range(4)]
    (
        row_sum, col_sum, inv_img, inv_mod, o_mod, o_low_img, o_low_mod, o_res_img, o_res_mod, o_power,
        o_weight,
        x_img, x_mod, w_img, w_mod, low_img, low_mod, res_img, res_mod, power, sems,
    ) = refs[20:]
    core, z, side = at[0], at[1], at[4]
    half, width = x_img.shape[1], x_img.shape[2]
    band, part = w_img.shape[2], half // 2
    size = 4 * half
    move = mover(sems)

    modal, image = [], []
    for kind, weights, needs in ((1, w_mod, modal), (0, w_img, image)):
        for own in range(2):
            c = core if own == 0 else 1 - core
            first, *others = met[2 * kind + own]
            blocks = [(first, 0), (others[0], 0)]
            blocks += [(one, i * (band + part)) for one in others[1:] for i in range(2)]
            for k, (block, start) in zip(meets(z, kind), blocks):
                needs.append(move(block.at[pl.ds(start, band)], weights.at[c, k]))
                to = x_mod.at[c * 8 + k, pl.ds(kind * part, part)]
                modal.append(move(block.at[pl.ds(start + band, part)], to))
    image.append(move(h_img, x_img))

    going = []
    for rows, w, low, rest, inverse, to, needs in (
        (x_mod, w_mod, low_mod, res_mod, inv_mod, (o_low_mod, o_res_mod), modal),
        (x_img, w_img, low_img, res_img, inv_img, (o_low_img, o_res_img), image),
    ):
        arrive(needs)
        if rows is x_mod:
            going.append(move(x_mod, o_mod))
        for i in range(4):
            take = slice(i * size, (i + 1) * size)
            proj = jnp.dot(
                rows[4 * i : 4 * i + 4].reshape(size, width),
                w[...].reshape(width, width),
                preferred_element_type=F32,
            )
            inv = lax.rsqrt(jnp.sum(proj * proj, axis=1, keepdims=True) + EPS)
            proj = proj * inv
            head = proj.astype(BF16)
            low[take] = head
            rest[take] = (proj - wider(head)).astype(BF16)
            inverse[:, take] = line(inv)
        going += [move(low, to[0]), move(rest, to[1])]

    own = sems.at[sems.shape[0] - 1]

    @pl.when(side == 0)
    def _():
        pltpu.make_async_copy(w_img, o_weight, own).start()

    @pl.when(side == 1)
    def _():
        pltpu.make_async_copy(w_mod, o_weight, own).start()

    factor = scale[0]
    cols = None
    for i in range(4):
        take = slice(i * size, (i + 1) * size)
        scores = lax.dot_general(
            low_img[take], low_mod[...], (((1,), (1,)), ((), ())), preferred_element_type=F32
        )
        value = jnp.exp(factor * scores)
        power[take] = value
        going.append(move(power.at[take], o_power.at[take]))
        fill(row_sum, line(jnp.sum(value, axis=1, keepdims=True)), i * size // 128)
        part = jnp.sum(value, axis=0, keepdims=True)
        cols = part if cols is None else cols + part
    fill(col_sum, cols, 0)
    arrive(going)
    pltpu.make_async_copy(w_img, o_weight, own).wait()


def gradient_kernel(
    at, scale, row_sum, col_sum, partner, inv_img, inv_mod,
    h_power, h_img, h_mod, h_low_img, h_low_mod, h_res_img, h_res_mod,
    o_img, o_keep, o_far, o_send,
    power, x_img, x_mod, low_img, low_mod, res_img, res_mod,
    weight_row, p_img, p_mod, keep, send, sems,
):
    core, z, y, x, side = [at[i] for i in range(5)]
    half, width = x_img.shape[1], x_img.shape[2]
    wide, band = width // 2, width // 16
    size = 4 * half
    factor = scale[0]
    move = mover(sems)
    parts = [slice(i * size, (i + 1) * size) for i in range(4)]

    def load(i):
        pairs = ((h_power, power), (h_low_img, low_img), (h_res_img, res_img))
        return [move(source.at[parts[i]], target.at[parts[i]]) for source, target in pairs]

    first = move(h_power.at[parts[0]], power.at[parts[0]])
    low = move(h_low_mod, low_mod)
    needs = [
        move(h_low_img.at[parts[0]], low_img.at[parts[0]]),
        move(h_res_img.at[parts[0]], res_img.at[parts[0]]),
    ]
    loads = [load(1)]

    j = lax.broadcasted_iota(jnp.int32, (1, 16 * half), 1)
    jz, jc, jr = (j // half) & 7, j // (8 * half), j & (half - 1)
    ids = ((((y // 2) * 8 + jz) * 4 + x) * 2 + jc) * (2 * half) + side * half + jr
    col = 1.0 / spread(col_sum)
    row = 1.0 / spread(row_sum)

    def weigh(i):
        take = parts[i]
        hit = column(partner[:, take]) == ids
        value = power[take] * (column(row[:, take]) + col)
        weight_row[take] = (value - jnp.where(hit, 2.0, 0.0)).astype(BF16)

    def tangent(grad, low, rest, inv):
        unit = wider(low) + wider(rest)
        along = jnp.sum(grad * unit, axis=1, keepdims=True)
        return (column(factor * inv) * (grad - unit * along)).astype(BF16).reshape(4, half, width)

    arrive([first])
    weigh(0)
    arrive([low] + needs)
    for i, take in enumerate(parts):
        if i < 2:
            loads.append(load(i + 2))
        if i == 2:
            modal = [move(h_res_mod, res_mod)]
            rest = [move(h_img, x_img), move(h_mod, x_mod)]
        if i < 3:
            arrive(loads[i])
        grad = jnp.dot(weight_row[take], low_mod[...], preferred_element_type=F32)
        if i < 3:
            weigh(i + 1)
        p_img[4 * i : 4 * i + 4] = tangent(grad, low_img[take], res_img[take], inv_img[:, take])
    going = [move(p_img, o_img)]
    arrive(modal)
    for i, take in enumerate(parts):
        grad = lax.dot_general(
            weight_row[:, take], low_img[...], (((0,), (0,)), ((), ())), preferred_element_type=F32
        )
        p_mod[4 * i : 4 * i + 4] = tangent(grad, low_mod[take], res_mod[take], inv_mod[:, take])
    part = half // 2
    block = band + part
    for kind in range(2):
        for i, k in enumerate(meets(z, kind)):
            keep[kind, i, band:] = p_mod[core * 8 + k, kind * part : (kind + 1) * part]
            send[kind, i, band:] = p_mod[(1 - core) * 8 + k, kind * part : (kind + 1) * part]
    arrive(rest)
    for kind, (rows, p) in enumerate(((x_img, p_img), (x_mod, p_mod))):
        for c in range(2):
            grad = lax.dot_general(
                rows[:, :, c * wide : (c + 1) * wide].reshape(16 * half, wide),
                p[...].reshape(16 * half, width),
                (((0,), (0,)), ((), ())),
                preferred_element_type=F32,
            ).astype(BF16)
            sign = 1 - 2 * ((z + kind) & 1)

            def put(target):
                for k in range(8):
                    step = (sign * (k - z)) & 7
                    at_step = jnp.where(step < 4, jnp.where(step < 2, step, step + 2), 9 - step)
                    at_step = jnp.where(step == 6, 3, jnp.where(step == 7, 2, at_step))
                    at_step = jnp.where(step == 5, 6, jnp.where(step == 4, 7, at_step))
                    target[kind, at_step, :band] = grad[k * band : (k + 1) * band]

            @pl.when(core == c)
            def _():
                put(keep)

            @pl.when(core != c)
            def _():
                put(send)

        going += [move(send.at[kind, pl.ds(6, 2)], o_far.at[kind])]
        going += [move(keep.at[kind], o_keep.at[kind]), move(send.at[kind], o_send.at[kind])]
    arrive(going)


def call(kernel, at, scale, operands, out, scratch, flops):
    spaces = {False: pl.BlockSpec(memory_space=pltpu.VMEM), True: pl.BlockSpec(memory_space=pl.ANY)}
    smem = pl.BlockSpec(memory_space=pltpu.SMEM)
    return pl.pallas_call(
        kernel,
        in_specs=[smem, smem] + [spaces[own] for _, own in operands],
        out_specs=[spaces[own] for _, own in out],
        out_shape=[jax.ShapeDtypeStruct(*one) for one, _ in out],
        scratch_shapes=[pltpu.VMEM(*one) for one in scratch] + [pltpu.SemaphoreType.DMA((96,))],
        compiler_params=pltpu.CompilerParams(vmem_limit_bytes=LIMIT),
        cost_estimate=pl.CostEstimate(flops=flops, bytes_accessed=8 << 20, transcendentals=0),
    )(at, scale, *[one for one, _ in operands])


def here_first(values, own):
    return [(one, own) for one in values]


def reorder(width):
    r = width // 128
    k = jnp.arange(width)
    low, c, x, z, yh = k % r, (k // r) % 2, (k // (2 * r)) % 4, (k // (8 * r)) % 8, k // (64 * r)
    to = (((c * 8 + z) * 2 + yh) * 4 + x) * r + low
    return (to[:, None] == k[None, :]).astype(BF16)


def per_device(embeds, weights, pair_index, scale):
    side = lax.axis_index("yl")
    yh, z, x, core = [lax.axis_index(name) for name in ROWS]
    at = jnp.stack([core, z, yh * 2 + side, x, side]).astype(jnp.int32)
    own, shard = embeds[0], weights[0]
    here, width = own.shape
    half, band, size = here // 2, 8 * shard.shape[0], 8 * here

    w0 = gather(shard, PLANE).reshape(2 * band, width)
    own = jnp.dot(own, reorder(width), preferred_element_type=F32).astype(BF16)

    keep = lax.dynamic_slice_in_dim(own, side * half, half, 0)
    send = lax.dynamic_slice_in_dim(own, (1 - side) * half, half, 0)
    came = mirror(send, ("yl",))
    image_x = jnp.where(side == 0, keep, came)
    modal_x = jnp.where(side == 0, came, keep)

    near = []
    for kind in range(2):
        rows = modal_x[kind * (half // 2) : (kind + 1) * (half // 2)]
        near.append([jnp.concatenate([w0[kind * band : (kind + 1) * band], rows])])
    far = [[mirror(one[0], ("c",))] for one in near]
    far[0][0], image_x = stage(far[0][0], image_x)
    image_x = gather(image_x, PLANE)
    for step in range(4):
        sent = [jnp.concatenate(one) if step == 1 else one[-1] for one in near]
        came = stage(*[pair(sent[kind], (kind + step) % 2) for kind in range(2)])
        for kind in range(2):
            near[kind].append(came[kind])
            far[kind].append(mirror(came[kind], ("c",)))
    pieces = [image_x, *near[0], *far[0], *near[1], *far[1]]

    table = pair_index.reshape(2, 8, 4, 2, 2, half)
    table = lax.dynamic_index_in_dim(table, z, 1, False)
    table = lax.dynamic_index_in_dim(table, core, 2, False)
    partner = table.transpose(2, 0, 1, 3).reshape(1, size)

    rows, flat = ((16, half, width), BF16), ((size, width), BF16)
    tile, one_line, square = ((8, size // 8), F32), ((1, size), F32), ((size, size), F32)
    some = ((2, 8, band, width), BF16)
    row_sum, col_sum, inv_img, inv_mod, x_mod, low_img, low_mod, res_img, res_mod, power, weight = call(
        score_kernel,
        at,
        scale,
        here_first(pieces, True),
        here_first([tile, tile, one_line, one_line], False) + here_first([rows, flat, flat, flat, flat, square, some], True),
        [rows, rows, some, some, flat, flat, flat, flat, square],
        4 * size * width * width + 2 * size * size * width,
    )
    for (axes, mask), (others, bit) in (
        ((("x",), 1), (("c",), 1)),
        ((("x",), 3), (("z",), 1)),
        ((Y, 2), (("z",), 2)),
        ((Y, 3), (("z",), 4)),
    ):
        row_sum, col_sum = stage(
            row_sum + mirror(row_sum, axes, mask), col_sum + mirror(col_sum, others, bit)
        )

    block = (2, 8, band + half // 2, width)
    some = (2, 2, band + half // 2, width)
    d_image, keep, far, send = call(
        gradient_kernel,
        at,
        scale,
        here_first([row_sum, col_sum, partner, inv_img, inv_mod], False)
        + here_first([power, image_x, x_mod, low_img, low_mod, res_img, res_mod], True),
        here_first([rows, (block, BF16), (some, BF16), (block, BF16)], True),
        [square, rows, rows, flat, flat, flat, flat, ((size, size), BF16), rows, rows]
        + [(block, BF16), (block, BF16)],
        4 * size * width * width + 4 * size * size * width,
    )
    far, send, d_image = stage(mirror(far, ("c",)), send, d_image)
    d_image = jnp.sum(wider(lax.all_to_all(d_image, PLANE, 0, 0)), axis=0)
    mine = [wider(keep[kind, 6:]) + wider(far[kind]) for kind in range(2)]
    came = [pair(mine[kind].astype(BF16), 1 - kind) for kind in range(2)]
    send = mirror(send, ("c",))
    *came, send = stage(*came, send)
    for step, first in ((1, 4), (2, 2)):
        take = slice(first, first + 2)
        mine = [wider(keep[kind, take]) + wider(send[kind, take]) + wider(came[kind]) for kind in range(2)]
        came = stage(*[pair(mine[kind].astype(BF16), (1 + kind + step) % 2) for kind in range(2)])
    mine = [wider(keep[kind, :2]) + wider(send[kind, :2]) + wider(came[kind]) for kind in range(2)]
    came = [pair(mine[kind][1].astype(BF16), kind) for kind in range(2)]
    sums = [mine[kind][0] + wider(came[kind]) for kind in range(2)]
    d_modal = jnp.concatenate([one[band:] for one in sums])
    d_weight = jnp.concatenate([one[:band] for one in sums]).reshape(16, band // 8, width)
    d_weight = jnp.sum(lax.all_to_all(d_weight, PLANE, 0, 0), axis=0)

    came = mirror(jnp.where(side == 0, d_modal, d_image), ("yl",))
    d_proj = jnp.where(
        side == 0,
        jnp.concatenate([d_image, came]),
        jnp.concatenate([came, d_modal]),
    ).astype(BF16)
    d_inputs = lax.dot_general(
        d_proj, weight.reshape(width, width), (((1,), (1,)), ((), ())), preferred_element_type=F32
    )
    d_inputs = lax.dot_general(
        d_inputs.astype(BF16), reorder(width), (((1,), (1,)), ((), ())), preferred_element_type=F32
    )
    return (d_inputs.astype(BF16)[None], d_weight[None])


def solution(mesh):
    devices = mesh.devices.reshape([SIZES[name] for name in AXES])
    return jax.shard_map(
        per_device,
        mesh=Mesh(devices, AXES),
        in_specs=(P("yl", ROWS, None), P("yl", ROWS, None), P(), P()),
        out_specs=(P("yl", ROWS, None), P("yl", ROWS, None)),
        check_vma=False,
    )
```

```python
import jax
import jax.numpy as jnp
from jax import lax
from jax.experimental import pallas as pl
from jax.experimental.pallas import tpu as pltpu
from jax.sharding import Mesh, PartitionSpec as P

EPS = 1e-06
AXES = ("yl", "yh", "z", "x", "c")
SIZES = {"yl": 2, "yh": 2, "z": 8, "x": 4, "c": 2}
ROWS = ("yh", "z", "x", "c")
PLANE = ("yl", "yh", "x")
Y = ("yl", "yh")
F32 = jnp.float32
BF16 = jnp.bfloat16
LIMIT = 56 << 20
MEET = (0, 1, -1, -2, 2, 3, -3, -4)


def count(axes):
    total = 1
    for name in axes:
        total *= SIZES[name]
    return total


def mirror(value, axes, mask=1):
    return lax.ppermute(value, axes, [(i, i ^ mask) for i in range(count(axes))])


def pair(value, step):
    size = SIZES["z"]
    route = []
    for i in range(size):
        for core in range(2):
            kind = (core + step) % 2
            other = (((i + kind) ^ 1) - kind) % size
            route.append((2 * i + core, 2 * other + core))
    return lax.ppermute(value, ("z", "c"), route)


def meets(z, core):
    sign = 1 - 2 * ((z + core) & 1)
    return [(z + sign * step) & 7 for step in MEET]


def gather(value, axes):
    copies = jnp.broadcast_to(value[None], (count(axes),) + value.shape)
    return lax.all_to_all(copies, axes, 0, 0)


def stage(*values):
    return lax.optimization_barrier(values)


def wider(value):
    return value.astype(F32)


def column(row):
    return jnp.transpose(jnp.broadcast_to(row, (128, row.shape[1])))[:, :1]


def line(values):
    return jnp.transpose(jnp.broadcast_to(values, (values.shape[0], 128)))[:1]


def mover(sems):
    used = []

    def move(source, target):
        copy = pltpu.make_async_copy(source, target, sems.at[len(used)])
        used.append(copy)
        copy.start()
        return copy

    return move


def arrive(copies):
    for copy in copies:
        copy.wait()


def fill(tile, values, first):
    for k in range(values.shape[1] // 128):
        tile[first + k : first + k + 1, :] = values[:, k * 128 : (k + 1) * 128]


def spread(tile):
    return jnp.concatenate([tile[k : k + 1, :] for k in range(tile.shape[0])], axis=1)


def score_kernel(at, scale, h_img, *refs):
    met = [refs[:4], refs[4:8]]
    (
        row_sum, col_sum, inv_img, inv_mod, o_mod, o_low_img, o_low_mod, o_res_img, o_res_mod, o_power,
        o_weight,
        x_img, x_mod, w_img, w_mod, low_img, low_mod, res_img, res_mod, power, sems,
    ) = refs[8:]
    core, z, side = at[0], at[1], at[4]
    half, width = x_img.shape[1], x_img.shape[2]
    band = w_img.shape[2]
    block = 2 * band + half
    size = 4 * half
    move = mover(sems)

    modal, image = [], []
    for want in range(2):
        for own in range(2):
            c = core if own == 0 else 1 - core
            for i, k in enumerate(meets(z, c)):
                piece, start = met[own][i // 2], (i % 2) * block
                if want == 0:
                    modal.append(move(piece.at[pl.ds(start + band, band)], w_mod.at[c, k]))
                    modal.append(move(piece.at[pl.ds(start + 2 * band, half)], x_mod.at[c * 8 + k]))
                else:
                    image.append(move(piece.at[pl.ds(start, band)], w_img.at[c, k]))
    image.append(move(h_img, x_img))

    going = []
    for rows, w, low, rest, inverse, to, needs in (
        (x_mod, w_mod, low_mod, res_mod, inv_mod, (o_low_mod, o_res_mod), modal),
        (x_img, w_img, low_img, res_img, inv_img, (o_low_img, o_res_img), image),
    ):
        arrive(needs)
        if rows is x_mod:
            going.append(move(x_mod, o_mod))
        for i in range(4):
            take = slice(i * size, (i + 1) * size)
            proj = jnp.dot(
                rows[4 * i : 4 * i + 4].reshape(size, width),
                w[...].reshape(width, width),
                preferred_element_type=F32,
            )
            inv = lax.rsqrt(jnp.sum(proj * proj, axis=1, keepdims=True) + EPS)
            proj = proj * inv
            head = proj.astype(BF16)
            low[take] = head
            rest[take] = (proj - wider(head)).astype(BF16)
            inverse[:, take] = line(inv)
        going += [move(low, to[0]), move(rest, to[1])]

    own = sems.at[sems.shape[0] - 1]

    @pl.when(side == 0)
    def _():
        pltpu.make_async_copy(w_img, o_weight, own).start()

    @pl.when(side == 1)
    def _():
        pltpu.make_async_copy(w_mod, o_weight, own).start()

    factor = scale[0]
    cols = None
    for i in range(4):
        take = slice(i * size, (i + 1) * size)
        scores = lax.dot_general(
            low_img[take], low_mod[...], (((1,), (1,)), ((), ())), preferred_element_type=F32
        )
        value = jnp.exp(factor * scores)
        power[take] = value
        going.append(move(power.at[take], o_power.at[take]))
        fill(row_sum, line(jnp.sum(value, axis=1, keepdims=True)), i * size // 128)
        part = jnp.sum(value, axis=0, keepdims=True)
        cols = part if cols is None else cols + part
    fill(col_sum, cols, 0)
    arrive(going)
    pltpu.make_async_copy(w_img, o_weight, own).wait()


def gradient_kernel(
    at, scale, row_sum, row_came, col_sum, col_came, partner, inv_img, inv_mod,
    h_power, h_img, h_mod, h_low_img, h_low_mod, h_res_img, h_res_mod,
    o_img, o_keep, o_send,
    power, x_img, x_mod, low_img, low_mod, res_img, res_mod,
    weight_row, p_img, p_mod, keep, send, sems,
):
    core, z, y, x, side = [at[i] for i in range(5)]
    half, width = x_img.shape[1], x_img.shape[2]
    wide, band = width // 2, width // 16
    size = 4 * half
    factor = scale[0]
    move = mover(sems)
    parts = [slice(i * size, (i + 1) * size) for i in range(4)]

    def load(i):
        pairs = ((h_power, power), (h_low_img, low_img), (h_res_img, res_img))
        return [move(source.at[parts[i]], target.at[parts[i]]) for source, target in pairs]

    first = move(h_power.at[parts[0]], power.at[parts[0]])
    low = move(h_low_mod, low_mod)
    needs = [
        move(h_low_img.at[parts[0]], low_img.at[parts[0]]),
        move(h_res_img.at[parts[0]], res_img.at[parts[0]]),
    ]
    loads = [load(1)]

    j = lax.broadcasted_iota(jnp.int32, (1, 16 * half), 1)
    jz, jc, jr = (j // half) & 7, j // (8 * half), j & (half - 1)
    ids = ((((y // 2) * 8 + jz) * 4 + x) * 2 + jc) * (2 * half) + side * half + jr
    col = 1.0 / spread(col_sum[...] + col_came[...])
    row = 1.0 / spread(row_sum[...] + row_came[...])

    def weigh(i):
        take = parts[i]
        hit = column(partner[:, take]) == ids
        value = power[take] * (column(row[:, take]) + col)
        weight_row[take] = (value - jnp.where(hit, 2.0, 0.0)).astype(BF16)

    def tangent(grad, low, rest, inv):
        unit = wider(low) + wider(rest)
        along = jnp.sum(grad * unit, axis=1, keepdims=True)
        return (column(factor * inv) * (grad - unit * along)).astype(BF16).reshape(4, half, width)

    arrive([first])
    weigh(0)
    arrive([low] + needs)
    for i, take in enumerate(parts):
        if i < 2:
            loads.append(load(i + 2))
        if i == 2:
            modal = [move(h_res_mod, res_mod)]
            rest = [move(h_img, x_img), move(h_mod, x_mod)]
        if i < 3:
            arrive(loads[i])
        grad = jnp.dot(weight_row[take], low_mod[...], preferred_element_type=F32)
        if i < 3:
            weigh(i + 1)
        p_img[4 * i : 4 * i + 4] = tangent(grad, low_img[take], res_img[take], inv_img[:, take])
    going = [move(p_img, o_img)]
    arrive(modal)
    for i, take in enumerate(parts):
        grad = lax.dot_general(
            weight_row[:, take], low_img[...], (((0,), (0,)), ((), ())), preferred_element_type=F32
        )
        p_mod[4 * i : 4 * i + 4] = tangent(grad, low_mod[take], res_mod[take], inv_mod[:, take])
    for c, target in ((core, keep), (1 - core, send)):
        for i, k in enumerate(meets(z, c)):
            target[i, 2 * band :] = p_mod[c * 8 + k]
    arrive(rest)
    for s, (rows, p) in enumerate(((x_img, p_img), (x_mod, p_mod))):
        lines = slice(s * band, (s + 1) * band)
        for c in range(2):
            grad = lax.dot_general(
                rows[:, :, c * wide : (c + 1) * wide].reshape(16 * half, wide),
                p[...].reshape(16 * half, width),
                (((0,), (0,)), ((), ())),
                preferred_element_type=F32,
            ).astype(BF16)
            sign = 1 - 2 * ((z + c) & 1)

            def put(target):
                for k in range(8):
                    step = (sign * (k - z)) & 7
                    spot = jnp.where(step < 2, step, jnp.where(step < 4, step + 2, 9 - step))
                    spot = jnp.where(step == 4, 7, jnp.where(step == 5, 6, spot))
                    target[spot, lines] = grad[k * band : (k + 1) * band]

            @pl.when(core == c)
            def _():
                put(keep)

            @pl.when(core != c)
            def _():
                put(send)

        if s == 0:
            first, last = pl.ds(0, band), pl.ds(2 * band, half)
            for source, target in ((keep, o_keep), (send, o_send)):
                for lines in (first, last):
                    going.append(move(source.at[pl.ds(0, 8), lines], target.at[pl.ds(0, 8), lines]))
        else:
            lines = pl.ds(band, band)
            for source, target in ((keep, o_keep), (send, o_send)):
                going.append(move(source.at[pl.ds(0, 8), lines], target.at[pl.ds(0, 8), lines]))
    arrive(going)


def call(kernel, at, scale, operands, out, scratch, flops):
    spaces = {False: pl.BlockSpec(memory_space=pltpu.VMEM), True: pl.BlockSpec(memory_space=pl.ANY)}
    smem = pl.BlockSpec(memory_space=pltpu.SMEM)
    return pl.pallas_call(
        kernel,
        in_specs=[smem, smem] + [spaces[own] for _, own in operands],
        out_specs=[spaces[own] for _, own in out],
        out_shape=[jax.ShapeDtypeStruct(*one) for one, _ in out],
        scratch_shapes=[pltpu.VMEM(*one) for one in scratch] + [pltpu.SemaphoreType.DMA((96,))],
        compiler_params=pltpu.CompilerParams(vmem_limit_bytes=LIMIT),
        cost_estimate=pl.CostEstimate(flops=flops, bytes_accessed=8 << 20, transcendentals=0),
    )(at, scale, *[one for one, _ in operands])


def here_first(values, own):
    return [(one, own) for one in values]


def reorder(width):
    r = width // 128
    k = jnp.arange(width)
    low, c, x, z, yh = k % r, (k // r) % 2, (k // (2 * r)) % 4, (k // (8 * r)) % 8, k // (64 * r)
    to = (((c * 8 + z) * 2 + yh) * 4 + x) * r + low
    return (to[:, None] == k[None, :]).astype(BF16)


def per_device(embeds, weights, pair_index, scale):
    side = lax.axis_index("yl")
    yh, z, x, core = [lax.axis_index(name) for name in ROWS]
    at = jnp.stack([core, z, yh * 2 + side, x, side]).astype(jnp.int32)
    own, shard = embeds[0], weights[0]
    here, width = own.shape
    half, band, size = here // 2, 8 * shard.shape[0], 8 * here

    w0 = gather(shard, PLANE).reshape(2 * band, width)
    own = jnp.dot(own, reorder(width), preferred_element_type=F32).astype(BF16)

    keep = lax.dynamic_slice_in_dim(own, side * half, half, 0)
    send = lax.dynamic_slice_in_dim(own, (1 - side) * half, half, 0)
    came = mirror(send, ("yl",))
    image_x = jnp.where(side == 0, keep, came)
    modal_x = jnp.where(side == 0, came, keep)

    copies = jnp.broadcast_to(image_x[None], (16, half, width))
    near = [jnp.concatenate([w0, modal_x])]
    near = [jnp.concatenate([near[0], pair(near[0], 0)])]
    far = [mirror(near[0], ("c",))]
    for step in (1, 2, 3):
        near.append(pair(near[-1], step))
        far.append(mirror(near[-1], ("c",)))
    image_x = lax.all_to_all(copies, PLANE, 0, 0)
    pieces = [image_x, *near, *far]

    table = pair_index.reshape(2, 8, 4, 2, 2, half)
    table = lax.dynamic_index_in_dim(table, z, 1, False)
    table = lax.dynamic_index_in_dim(table, core, 2, False)
    partner = table.transpose(2, 0, 1, 3).reshape(1, size)

    rows, flat = ((16, half, width), BF16), ((size, width), BF16)
    tile, one_line, square = ((8, size // 8), F32), ((1, size), F32), ((size, size), F32)
    some = ((2, 8, band, width), BF16)
    row_sum, col_sum, inv_img, inv_mod, x_mod, low_img, low_mod, res_img, res_mod, power, weight = call(
        score_kernel,
        at,
        scale,
        here_first(pieces, True),
        here_first([tile, tile, one_line, one_line], False) + here_first([rows, flat, flat, flat, flat, square, some], True),
        [rows, rows, some, some, flat, flat, flat, flat, square],
        4 * size * width * width + 2 * size * size * width,
    )
    def exchange(row_sum, col_sum, step):
        axes, mask = ((("x",), 1), (("x",), 3), (Y, 2), (Y, 3))[step]
        if step == 0:
            came = mirror(col_sum, ("c",))
        elif step == 3:
            came = mirror(col_sum, ("z",), 4)
        else:
            came = pair(col_sum, step)
        return stage(mirror(row_sum, axes, mask), came)

    for step in range(3):
        row_came, col_came = exchange(row_sum, col_sum, step)
        row_sum, col_sum = row_sum + row_came, col_sum + col_came
    row_came, col_came = exchange(row_sum, col_sum, 3)

    block = (8, 2 * band + half, width)
    d_image, keep, send = call(
        gradient_kernel,
        at,
        scale,
        here_first([row_sum, row_came, col_sum, col_came, partner, inv_img, inv_mod], False)
        + here_first([power, image_x, x_mod, low_img, low_mod, res_img, res_mod], True),
        here_first([rows, (block, BF16), (block, BF16)], True),
        [square, rows, rows, flat, flat, flat, flat, ((size, size), BF16), rows, rows]
        + [(block, BF16), (block, BF16)],
        4 * size * width * width + 4 * size * size * width,
    )
    d_image = jnp.sum(wider(lax.all_to_all(d_image, PLANE, 0, 0)), axis=0)
    send = mirror(send, ("c",))
    mine = wider(keep[6:]) + wider(send[6:])
    for step, first in ((1, 4), (0, 2), (1, 0)):
        came = pair(mine.astype(BF16), step)
        mine = wider(keep[first : first + 2]) + wider(send[first : first + 2]) + wider(came)
    sums = mine[0] + wider(pair(mine[1].astype(BF16), 0))
    d_modal = sums[2 * band :]
    d_weight = sums[: 2 * band].reshape(16, band // 8, width)
    d_weight = jnp.sum(lax.all_to_all(d_weight, PLANE, 0, 0), axis=0)

    came = mirror(jnp.where(side == 0, d_modal, d_image), ("yl",))
    d_proj = jnp.where(
        side == 0,
        jnp.concatenate([d_image, came]),
        jnp.concatenate([came, d_modal]),
    ).astype(BF16)
    d_inputs = lax.dot_general(
        d_proj, weight.reshape(width, width), (((1,), (1,)), ((), ())), preferred_element_type=F32
    )
    d_inputs = lax.dot_general(
        d_inputs.astype(BF16), reorder(width), (((1,), (1,)), ((), ())), preferred_element_type=F32
    )
    return (d_inputs.astype(BF16)[None], d_weight[None])


def solution(mesh):
    devices = mesh.devices.reshape([SIZES[name] for name in AXES])
    return jax.shard_map(
        per_device,
        mesh=Mesh(devices, AXES),
        in_specs=(P("yl", ROWS, None), P("yl", ROWS, None), P(), P()),
        out_specs=(P("yl", ROWS, None), P("yl", ROWS, None)),
        check_vma=False,
    )
```

```python
import jax
import jax.numpy as jnp
from jax import lax
from jax.experimental import pallas as pl
from jax.experimental.pallas import tpu as pltpu
from jax.sharding import Mesh, PartitionSpec as P

EPS = 1e-06
AXES = ("yl", "yh", "z", "x", "c")
SIZES = {"yl": 2, "yh": 2, "z": 8, "x": 4, "c": 2}
ROWS = ("yh", "z", "x", "c")
PLANE = ("yl", "yh", "x")
Y = ("yl", "yh")
F32 = jnp.float32
BF16 = jnp.bfloat16
LIMIT = 52 << 20
MEET = (0, 1, -1, -2, 2, 3, -3, -4)


def count(axes):
    total = 1
    for name in axes:
        total *= SIZES[name]
    return total


def mirror(value, axes, mask=1):
    return lax.ppermute(value, axes, [(i, i ^ mask) for i in range(count(axes))])


def pair(value, step):
    size = SIZES["z"]
    route = []
    for i in range(size):
        for core in range(2):
            kind = (core + step) % 2
            other = (((i + kind) ^ 1) - kind) % size
            route.append((2 * i + core, 2 * other + core))
    return lax.ppermute(value, ("z", "c"), route)


def meets(z, core):
    sign = 1 - 2 * ((z + core) & 1)
    return [(z + sign * step) & 7 for step in MEET]


def gather(value, axes):
    copies = jnp.broadcast_to(value[None], (count(axes),) + value.shape)
    return lax.all_to_all(copies, axes, 0, 0)


def stage(*values):
    return lax.optimization_barrier(values)


def wider(value):
    return value.astype(F32)


def column(row):
    return jnp.transpose(jnp.broadcast_to(row, (128, row.shape[1])))[:, :1]


def line(values):
    return jnp.transpose(jnp.broadcast_to(values, (values.shape[0], 128)))[:1]


def mover(sems):
    used = []

    def move(source, target):
        copy = pltpu.make_async_copy(source, target, sems.at[len(used)])
        used.append(copy)
        copy.start()
        return copy

    return move


def arrive(copies):
    for copy in copies:
        copy.wait()


def fill(tile, values, first):
    for k in range(values.shape[1] // 128):
        tile[first + k : first + k + 1, :] = values[:, k * 128 : (k + 1) * 128]


def spread(tile):
    return jnp.concatenate([tile[k : k + 1, :] for k in range(tile.shape[0])], axis=1)


def score_kernel(at, scale, h_img, *refs):
    met = [refs[:4], refs[4:8]]
    (
        row_sum, col_sum, inv_img, inv_mod, o_mod, o_low_img, o_low_mod, o_res_img, o_res_mod, o_power,
        o_weight,
        x_img, x_mod, w_img, w_mod, low_img, low_mod, res_img, res_mod, power, sems,
    ) = refs[8:]
    core, z, side = at[0], at[1], at[4]
    half, width = x_img.shape[1], x_img.shape[2]
    band = w_img.shape[2]
    block = 2 * band + half
    size = 4 * half
    move = mover(sems)

    modal, image = [], []
    image.append(move(h_img, x_img))
    for want in (0, 1):
        for own in range(2):
            c = core if own == 0 else 1 - core
            for i, k in enumerate(meets(z, c)):
                piece, start = met[own][i // 2], (i % 2) * block
                if want == 0:
                    modal.append(move(piece.at[pl.ds(start + band, band)], w_mod.at[c, k]))
                    modal.append(move(piece.at[pl.ds(start + 2 * band, half)], x_mod.at[c * 8 + k]))
                else:
                    image.append(move(piece.at[pl.ds(start, band)], w_img.at[c, k]))

    going = []
    for rows, w, low, rest, inverse, to, needs in (
        (x_mod, w_mod, low_mod, res_mod, inv_mod, (o_low_mod, o_res_mod), modal),
        (x_img, w_img, low_img, res_img, inv_img, (o_low_img, o_res_img), image),
    ):
        arrive(needs)
        if rows is x_mod:
            going.append(move(x_mod, o_mod))
        for i in range(4):
            take = slice(i * size, (i + 1) * size)
            proj = jnp.dot(
                rows[4 * i : 4 * i + 4].reshape(size, width),
                w[...].reshape(width, width),
                preferred_element_type=F32,
            )
            inv = lax.rsqrt(jnp.sum(proj * proj, axis=1, keepdims=True) + EPS)
            proj = proj * inv
            head = proj.astype(BF16)
            low[take] = head
            rest[take] = (proj - wider(head)).astype(BF16)
            inverse[:, take] = line(inv)
        going += [move(low, to[0]), move(rest, to[1])]

    own = sems.at[sems.shape[0] - 1]

    @pl.when(side == 0)
    def _():
        pltpu.make_async_copy(w_img, o_weight, own).start()

    @pl.when(side == 1)
    def _():
        pltpu.make_async_copy(w_mod, o_weight, own).start()

    factor = scale[0]
    cols = None
    for i in range(4):
        take = slice(i * size, (i + 1) * size)
        scores = lax.dot_general(
            low_img[take], low_mod[...], (((1,), (1,)), ((), ())), preferred_element_type=F32
        )
        value = jnp.exp(factor * scores)
        power[take] = value
        going.append(move(power.at[take], o_power.at[take]))
        fill(row_sum, line(jnp.sum(value, axis=1, keepdims=True)), i * size // 128)
        part = jnp.sum(value, axis=0, keepdims=True)
        cols = part if cols is None else cols + part
    fill(col_sum, cols, 0)
    arrive(going)
    pltpu.make_async_copy(w_img, o_weight, own).wait()


def gradient_kernel(
    at, scale, row_sum, row_came, col_sum, col_came, partner, inv_img, inv_mod,
    h_power, h_img, h_mod, h_low_img, h_low_mod, h_res_img, h_res_mod,
    o_img, o_keep, o_far, o_send,
    power, x_img, x_mod, low_img, low_mod, res_img, res_mod,
    weight_row, p_img, p_mod, keep, send, sems,
):
    core, z, y, x, side = [at[i] for i in range(5)]
    half, width = x_img.shape[1], x_img.shape[2]
    wide, band = width // 2, width // 16
    size = 4 * half
    factor = scale[0]
    move = mover(sems)
    parts = [slice(i * size, (i + 1) * size) for i in range(4)]

    def load(i):
        pairs = ((h_power, power), (h_low_img, low_img), (h_res_img, res_img))
        return [move(source.at[parts[i]], target.at[parts[i]]) for source, target in pairs]

    first = move(h_power.at[parts[0]], power.at[parts[0]])
    low = move(h_low_mod, low_mod)
    needs = [
        move(h_low_img.at[parts[0]], low_img.at[parts[0]]),
        move(h_res_img.at[parts[0]], res_img.at[parts[0]]),
    ]
    loads = [load(1), load(2), load(3)]
    modal = [move(h_res_mod, res_mod)]
    rest = [move(h_img, x_img), move(h_mod, x_mod)]

    j = lax.broadcasted_iota(jnp.int32, (1, 16 * half), 1)
    jz, jc, jr = (j // half) & 7, j // (8 * half), j & (half - 1)
    ids = ((((y // 2) * 8 + jz) * 4 + x) * 2 + jc) * (2 * half) + side * half + jr
    col = 1.0 / spread(col_sum[...] + col_came[...])
    row = 1.0 / spread(row_sum[...] + row_came[...])

    def weigh(i):
        take = parts[i]
        hit = column(partner[:, take]) == ids
        value = power[take] * (column(row[:, take]) + col)
        weight_row[take] = (value - jnp.where(hit, 2.0, 0.0)).astype(BF16)

    def tangent(grad, low, rest, inv):
        unit = wider(low) + wider(rest)
        along = jnp.sum(grad * unit, axis=1, keepdims=True)
        return (column(factor * inv) * (grad - unit * along)).astype(BF16).reshape(4, half, width)

    arrive([first])
    weigh(0)
    arrive([low] + needs)
    for i, take in enumerate(parts):
        if i < 3:
            arrive(loads[i])
        grad = jnp.dot(weight_row[take], low_mod[...], preferred_element_type=F32)
        if i < 3:
            weigh(i + 1)
        p_img[4 * i : 4 * i + 4] = tangent(grad, low_img[take], res_img[take], inv_img[:, take])
    going = [move(p_img, o_img)]
    arrive(modal)
    for i, take in enumerate(parts):
        grad = lax.dot_general(
            weight_row[:, take], low_img[...], (((0,), (0,)), ((), ())), preferred_element_type=F32
        )
        p_mod[4 * i : 4 * i + 4] = tangent(grad, low_mod[take], res_mod[take], inv_mod[:, take])
    for c, target in ((core, keep), (1 - core, send)):
        for i, k in enumerate(meets(z, c)):
            target[i, 2 * band :] = p_mod[c * 8 + k]
    arrive(rest)
    for s, (rows, p) in enumerate(((x_img, p_img), (x_mod, p_mod))):
        lines = slice(s * band, (s + 1) * band)
        for c in range(2):
            grad = lax.dot_general(
                rows[:, :, c * wide : (c + 1) * wide].reshape(16 * half, wide),
                p[...].reshape(16 * half, width),
                (((0,), (0,)), ((), ())),
                preferred_element_type=F32,
            ).astype(BF16)
            sign = 1 - 2 * ((z + c) & 1)

            def put(target):
                for k in range(8):
                    step = (sign * (k - z)) & 7
                    spot = jnp.where(step < 2, step, jnp.where(step < 4, step + 2, 9 - step))
                    spot = jnp.where(step == 4, 7, jnp.where(step == 5, 6, spot))
                    target[spot, lines] = grad[k * band : (k + 1) * band]

            @pl.when(core == c)
            def _():
                put(keep)

            @pl.when(core != c)
            def _():
                put(send)

        for lines in (pl.ds(0, band), pl.ds(2 * band, half)) if s == 0 else (pl.ds(band, band),):
            for source, target in ((keep, o_keep), (send, o_send)):
                going.append(move(source.at[pl.ds(0, 8), lines], target.at[pl.ds(0, 8), lines]))
            going.append(move(send.at[pl.ds(6, 2), lines], o_far.at[pl.ds(0, 2), lines]))
    arrive(going)


def call(kernel, at, scale, operands, out, scratch, flops):
    spaces = {False: pl.BlockSpec(memory_space=pltpu.VMEM), True: pl.BlockSpec(memory_space=pl.ANY)}
    smem = pl.BlockSpec(memory_space=pltpu.SMEM)
    return pl.pallas_call(
        kernel,
        in_specs=[smem, smem] + [spaces[own] for _, own in operands],
        out_specs=[spaces[own] for _, own in out],
        out_shape=[jax.ShapeDtypeStruct(*one) for one, _ in out],
        scratch_shapes=[pltpu.VMEM(*one) for one in scratch] + [pltpu.SemaphoreType.DMA((96,))],
        compiler_params=pltpu.CompilerParams(vmem_limit_bytes=LIMIT),
        cost_estimate=pl.CostEstimate(flops=flops, bytes_accessed=8 << 20, transcendentals=0),
    )(at, scale, *[one for one, _ in operands])


def here_first(values, own):
    return [(one, own) for one in values]


def reorder(width):
    r = width // 128
    k = jnp.arange(width)
    low, c, x, z, yh = k % r, (k // r) % 2, (k // (2 * r)) % 4, (k // (8 * r)) % 8, k // (64 * r)
    to = (((c * 8 + z) * 2 + yh) * 4 + x) * r + low
    return (to[:, None] == k[None, :]).astype(BF16)


def per_device(embeds, weights, pair_index, scale):
    side = lax.axis_index("yl")
    yh, z, x, core = [lax.axis_index(name) for name in ROWS]
    at = jnp.stack([core, z, yh * 2 + side, x, side]).astype(jnp.int32)
    own, shard = embeds[0], weights[0]
    here, width = own.shape
    half, band, size = here // 2, 8 * shard.shape[0], 8 * here

    w0 = gather(shard, PLANE).reshape(2 * band, width)
    own = jnp.dot(own, reorder(width), preferred_element_type=F32).astype(BF16)

    keep = lax.dynamic_slice_in_dim(own, side * half, half, 0)
    send = lax.dynamic_slice_in_dim(own, (1 - side) * half, half, 0)
    came = mirror(send, ("yl",))
    image_x = jnp.where(side == 0, keep, came)
    modal_x = jnp.where(side == 0, came, keep)

    copies = jnp.broadcast_to(image_x[None], (16, half, width))
    near = [jnp.concatenate([w0, modal_x])]
    near = [jnp.concatenate([near[0], pair(near[0], 0)])]
    far = [mirror(near[0], ("c",))]
    for step in (1, 2, 3):
        near.append(pair(near[-1], step))
        far.append(mirror(near[-1], ("c",)))
    image_x = lax.all_to_all(copies, PLANE, 0, 0)
    pieces = [image_x, *near, *far]

    table = pair_index.reshape(2, 8, 4, 2, 2, half)
    table = lax.dynamic_index_in_dim(table, z, 1, False)
    table = lax.dynamic_index_in_dim(table, core, 2, False)
    partner = table.transpose(2, 0, 1, 3).reshape(1, size)

    rows, flat = ((16, half, width), BF16), ((size, width), BF16)
    tile, one_line, square = ((8, size // 8), F32), ((1, size), F32), ((size, size), F32)
    some = ((2, 8, band, width), BF16)
    row_sum, col_sum, inv_img, inv_mod, x_mod, low_img, low_mod, res_img, res_mod, power, weight = call(
        score_kernel,
        at,
        scale,
        here_first(pieces, True),
        here_first([tile, tile, one_line, one_line], False) + here_first([rows, flat, flat, flat, flat, square, some], True),
        [rows, rows, some, some, flat, flat, flat, flat, square],
        4 * size * width * width + 2 * size * size * width,
    )
    def exchange(row_sum, col_sum, step):
        axes, mask = ((("x",), 1), (("x",), 3), (Y, 2), (Y, 3))[step]
        if step == 0:
            came = mirror(col_sum, ("c",))
        elif step == 3:
            came = mirror(col_sum, ("z",), 4)
        else:
            came = pair(col_sum, step)
        return stage(mirror(row_sum, axes, mask), came)

    for step in range(3):
        row_came, col_came = exchange(row_sum, col_sum, step)
        row_sum, col_sum = row_sum + row_came, col_sum + col_came
    row_came, col_came = exchange(row_sum, col_sum, 3)

    block = (8, 2 * band + half, width)
    d_image, keep, far, send = call(
        gradient_kernel,
        at,
        scale,
        here_first([row_sum, row_came, col_sum, col_came, partner, inv_img, inv_mod], False)
        + here_first([power, image_x, x_mod, low_img, low_mod, res_img, res_mod], True),
        here_first([rows, (block, BF16), ((2, *block[1:]), BF16), (block, BF16)], True),
        [square, rows, rows, flat, flat, flat, flat, ((size, size), BF16), rows, rows]
        + [(block, BF16), (block, BF16)],
        4 * size * width * width + 4 * size * size * width,
    )
    d_image = lax.all_to_all(d_image, PLANE, 0, 0)
    far, send = stage(mirror(far, ("c",)), send)
    mine = wider(keep[6:]) + wider(far)
    send = mirror(send, ("c",))
    for step, first in ((1, 4), (0, 2), (1, 0)):
        came = pair(mine.astype(BF16), step)
        if first == 0:
            came, d_image = stage(came, d_image)
        mine = wider(keep[first : first + 2]) + wider(send[first : first + 2]) + wider(came)
    sums = mine[0] + wider(pair(mine[1].astype(BF16), 0))
    d_image = jnp.sum(wider(d_image), axis=0)
    d_modal = sums[2 * band :]
    d_weight = sums[: 2 * band].reshape(16, band // 8, width)
    d_weight = jnp.sum(lax.all_to_all(d_weight, PLANE, 0, 0), axis=0, keepdims=True)

    came = mirror(jnp.where(side == 0, d_modal, d_image), ("yl",))
    d_proj = jnp.where(
        side == 0,
        jnp.concatenate([d_image, came]),
        jnp.concatenate([came, d_modal]),
    ).astype(BF16)
    d_inputs = lax.dot_general(
        d_proj, weight.reshape(width, width), (((1,), (1,)), ((), ())), preferred_element_type=F32
    )
    d_inputs = lax.dot_general(
        d_inputs.astype(BF16), reorder(width), (((1,), (1,)), ((), ())), preferred_element_type=F32
    )
    return (d_inputs.astype(BF16)[None], d_weight)


def solution(mesh):
    devices = mesh.devices.reshape([SIZES[name] for name in AXES])
    return jax.shard_map(
        per_device,
        mesh=Mesh(devices, AXES),
        in_specs=(P("yl", ROWS, None), P("yl", ROWS, None), P(), P()),
        out_specs=(P("yl", ROWS, None), P("yl", ROWS, None)),
        check_vma=False,
    )
```

```python
import jax
import jax.numpy as jnp
from jax import lax
from jax.experimental import pallas as pl
from jax.experimental.pallas import tpu as pltpu
from jax.sharding import Mesh, PartitionSpec as P

EPS = 1e-06
AXES = ("yl", "yh", "z", "x", "c")
SIZES = {"yl": 2, "yh": 2, "z": 8, "x": 4, "c": 2}
ROWS = ("yh", "z", "x", "c")
PLANE = ("yl", "yh", "x")
Y = ("yl", "yh")
F32 = jnp.float32
BF16 = jnp.bfloat16
LIMIT = 52 << 20
MEET = (0, 1, -1, -2, 2, 3, -3, -4)


def count(axes):
    total = 1
    for name in axes:
        total *= SIZES[name]
    return total


def mirror(value, axes, mask=1):
    return lax.ppermute(value, axes, [(i, i ^ mask) for i in range(count(axes))])


def pair(value, step):
    size = SIZES["z"]
    route = []
    for i in range(size):
        for core in range(2):
            kind = (core + step) % 2
            other = (((i + kind) ^ 1) - kind) % size
            route.append((2 * i + core, 2 * other + core))
    return lax.ppermute(value, ("z", "c"), route)


def across(value):
    size = SIZES["z"]
    route = []
    for i in range(size):
        for core in range(2):
            step = 3 if (i + core) % 2 else -3
            route.append((2 * i + core, 2 * ((i + step) % size) + core))
    return lax.ppermute(value, ("z", "c"), route)


def meets(z, core):
    sign = 1 - 2 * ((z + core) & 1)
    return [(z + sign * step) & 7 for step in MEET]


def gather(value, axes):
    copies = jnp.broadcast_to(value[None], (count(axes),) + value.shape)
    return lax.all_to_all(copies, axes, 0, 0)


def stage(*values):
    return lax.optimization_barrier(values)


def wider(value):
    return value.astype(F32)


def column(row):
    return jnp.transpose(jnp.broadcast_to(row, (128, row.shape[1])))[:, :1]


def line(values):
    return jnp.transpose(jnp.broadcast_to(values, (values.shape[0], 128)))[:1]


def mover(sems):
    used = []

    def move(source, target):
        copy = pltpu.make_async_copy(source, target, sems.at[len(used)])
        used.append(copy)
        copy.start()
        return copy

    return move


def arrive(copies):
    for copy in copies:
        copy.wait()


def fill(tile, values, first):
    for k in range(values.shape[1] // 128):
        tile[first + k : first + k + 1, :] = values[:, k * 128 : (k + 1) * 128]


def spread(tile):
    return jnp.concatenate([tile[k : k + 1, :] for k in range(tile.shape[0])], axis=1)


def score_kernel(at, scale, h_img, *refs):
    met = [refs[:4], refs[4:8]]
    (
        row_sum, col_sum, inv_img, inv_mod, o_mod, o_low_img, o_low_mod, o_res_img, o_res_mod, o_power,
        o_weight,
        x_img, x_mod, w_img, w_mod, low_img, low_mod, res_img, res_mod, power, sems,
    ) = refs[8:]
    core, z, side = at[0], at[1], at[4]
    half, width = x_img.shape[1], x_img.shape[2]
    band = w_img.shape[2]
    block = 2 * band + half
    size = 4 * half
    move = mover(sems)

    modal, image = [], []
    image.append(move(h_img, x_img))
    for want in (0, 1):
        for own in range(2):
            c = core if own == 0 else 1 - core
            for i, k in enumerate(meets(z, c)):
                piece, start = met[own][i // 2], (i % 2) * block
                if want == 0:
                    modal.append(move(piece.at[pl.ds(start + band, band)], w_mod.at[c, k]))
                    modal.append(move(piece.at[pl.ds(start + 2 * band, half)], x_mod.at[c * 8 + k]))
                else:
                    image.append(move(piece.at[pl.ds(start, band)], w_img.at[c, k]))

    going = []
    for rows, w, low, rest, inverse, to, needs in (
        (x_mod, w_mod, low_mod, res_mod, inv_mod, (o_low_mod, o_res_mod), modal),
        (x_img, w_img, low_img, res_img, inv_img, (o_low_img, o_res_img), image),
    ):
        arrive(needs)
        if rows is x_mod:
            going.append(move(x_mod, o_mod))
        for i in range(4):
            take = slice(i * size, (i + 1) * size)
            proj = jnp.dot(
                rows[4 * i : 4 * i + 4].reshape(size, width),
                w[...].reshape(width, width),
                preferred_element_type=F32,
            )
            inv = lax.rsqrt(jnp.sum(proj * proj, axis=1, keepdims=True) + EPS)
            proj = proj * inv
            head = proj.astype(BF16)
            low[take] = head
            rest[take] = (proj - wider(head)).astype(BF16)
            inverse[:, take] = line(inv)
        going += [move(low, to[0]), move(rest, to[1])]

    own = sems.at[sems.shape[0] - 1]

    @pl.when(side == 0)
    def _():
        pltpu.make_async_copy(w_img, o_weight, own).start()

    @pl.when(side == 1)
    def _():
        pltpu.make_async_copy(w_mod, o_weight, own).start()

    factor = scale[0]
    cols = None
    for i in range(4):
        take = slice(i * size, (i + 1) * size)
        scores = lax.dot_general(
            low_img[take], low_mod[...], (((1,), (1,)), ((), ())), preferred_element_type=F32
        )
        value = jnp.exp(factor * scores)
        power[take] = value
        going.append(move(power.at[take], o_power.at[take]))
        fill(row_sum, line(jnp.sum(value, axis=1, keepdims=True)), i * size // 128)
        part = jnp.sum(value, axis=0, keepdims=True)
        cols = part if cols is None else cols + part
    fill(col_sum, cols, 0)
    arrive(going)
    pltpu.make_async_copy(w_img, o_weight, own).wait()


def gradient_kernel(
    at, scale, row_sum, row_came, col_sum, col_came, partner, inv_img, inv_mod,
    h_power, h_img, h_mod, h_low_img, h_low_mod, h_res_img, h_res_mod,
    o_img, o_keep, o_far, o_send,
    power, x_img, x_mod, low_img, low_mod, res_img, res_mod,
    weight_row, p_img, p_mod, keep, send, sems,
):
    core, z, y, x, side = [at[i] for i in range(5)]
    half, width = x_img.shape[1], x_img.shape[2]
    wide, band = width // 2, width // 16
    size = 4 * half
    factor = scale[0]
    move = mover(sems)
    parts = [slice(i * size, (i + 1) * size) for i in range(4)]

    def load(i):
        pairs = ((h_power, power), (h_low_img, low_img), (h_res_img, res_img))
        return [move(source.at[parts[i]], target.at[parts[i]]) for source, target in pairs]

    first = move(h_power.at[parts[0]], power.at[parts[0]])
    low = move(h_low_mod, low_mod)
    needs = [
        move(h_low_img.at[parts[0]], low_img.at[parts[0]]),
        move(h_res_img.at[parts[0]], res_img.at[parts[0]]),
    ]
    loads = [load(1), load(2), load(3)]
    modal = [move(h_res_mod, res_mod)]
    rest = [move(h_img, x_img), move(h_mod, x_mod)]

    j = lax.broadcasted_iota(jnp.int32, (1, 16 * half), 1)
    jz, jc, jr = (j // half) & 7, j // (8 * half), j & (half - 1)
    ids = ((((y // 2) * 8 + jz) * 4 + x) * 2 + jc) * (2 * half) + side * half + jr
    col = 1.0 / spread(col_sum[...] + col_came[...])
    row = 1.0 / spread(row_sum[...] + row_came[...])

    def weigh(i):
        take = parts[i]
        hit = column(partner[:, take]) == ids
        value = power[take] * (column(row[:, take]) + col)
        weight_row[take] = (value - jnp.where(hit, 2.0, 0.0)).astype(BF16)

    def tangent(grad, low, rest, inv):
        unit = wider(low) + wider(rest)
        along = jnp.sum(grad * unit, axis=1, keepdims=True)
        return (column(factor * inv) * (grad - unit * along)).astype(BF16).reshape(4, half, width)

    arrive([first])
    weigh(0)
    arrive([low] + needs)
    for i, take in enumerate(parts):
        if i < 3:
            arrive(loads[i])
        grad = jnp.dot(weight_row[take], low_mod[...], preferred_element_type=F32)
        if i < 3:
            weigh(i + 1)
        p_img[4 * i : 4 * i + 4] = tangent(grad, low_img[take], res_img[take], inv_img[:, take])
    going = [move(p_img, o_img)]
    arrive(modal)
    for i, take in enumerate(parts):
        grad = lax.dot_general(
            weight_row[:, take], low_img[...], (((0,), (0,)), ((), ())), preferred_element_type=F32
        )
        p_mod[4 * i : 4 * i + 4] = tangent(grad, low_mod[take], res_mod[take], inv_mod[:, take])
    for c, target in ((core, keep), (1 - core, send)):
        for i, k in enumerate(meets(z, c)):
            target[i, 2 * band :] = p_mod[c * 8 + k]
    arrive(rest)
    for s, (rows, p) in enumerate(((x_img, p_img), (x_mod, p_mod))):
        lines = slice(s * band, (s + 1) * band)
        for c in range(2):
            grad = lax.dot_general(
                rows[:, :, c * wide : (c + 1) * wide].reshape(16 * half, wide),
                p[...].reshape(16 * half, width),
                (((0,), (0,)), ((), ())),
                preferred_element_type=F32,
            ).astype(BF16)
            sign = 1 - 2 * ((z + c) & 1)

            def put(target):
                for k in range(8):
                    step = (sign * (k - z)) & 7
                    spot = jnp.where(step < 2, step, jnp.where(step < 4, step + 2, 9 - step))
                    spot = jnp.where(step == 4, 7, jnp.where(step == 5, 6, spot))
                    target[spot, lines] = grad[k * band : (k + 1) * band]

            @pl.when(core == c)
            def _():
                put(keep)

            @pl.when(core != c)
            def _():
                put(send)

        for lines in (pl.ds(0, band), pl.ds(2 * band, half)) if s == 0 else (pl.ds(band, band),):
            for source, target in ((keep, o_keep), (send, o_send)):
                going.append(move(source.at[pl.ds(0, 8), lines], target.at[pl.ds(0, 8), lines]))
            going.append(move(send.at[pl.ds(6, 2), lines], o_far.at[pl.ds(0, 2), lines]))
    arrive(going)


def call(kernel, at, scale, operands, out, scratch, flops):
    spaces = {False: pl.BlockSpec(memory_space=pltpu.VMEM), True: pl.BlockSpec(memory_space=pl.ANY)}
    smem = pl.BlockSpec(memory_space=pltpu.SMEM)
    return pl.pallas_call(
        kernel,
        in_specs=[smem, smem] + [spaces[own] for _, own in operands],
        out_specs=[spaces[own] for _, own in out],
        out_shape=[jax.ShapeDtypeStruct(*one) for one, _ in out],
        scratch_shapes=[pltpu.VMEM(*one) for one in scratch] + [pltpu.SemaphoreType.DMA((96,))],
        compiler_params=pltpu.CompilerParams(vmem_limit_bytes=LIMIT),
        cost_estimate=pl.CostEstimate(flops=flops, bytes_accessed=8 << 20, transcendentals=0),
    )(at, scale, *[one for one, _ in operands])


def here_first(values, own):
    return [(one, own) for one in values]


def reorder(width):
    r = width // 128
    k = jnp.arange(width)
    low, c, x, z, yh = k % r, (k // r) % 2, (k // (2 * r)) % 4, (k // (8 * r)) % 8, k // (64 * r)
    to = (((c * 8 + z) * 2 + yh) * 4 + x) * r + low
    return (to[:, None] == k[None, :]).astype(BF16)


def per_device(embeds, weights, pair_index, scale):
    side = lax.axis_index("yl")
    yh, z, x, core = [lax.axis_index(name) for name in ROWS]
    at = jnp.stack([core, z, yh * 2 + side, x, side]).astype(jnp.int32)
    own, shard = embeds[0], weights[0]
    here, width = own.shape
    half, band, size = here // 2, 8 * shard.shape[0], 8 * here

    w0 = gather(shard, PLANE).reshape(2 * band, width)
    own = jnp.dot(own, reorder(width), preferred_element_type=F32).astype(BF16)

    keep = lax.dynamic_slice_in_dim(own, side * half, half, 0)
    send = lax.dynamic_slice_in_dim(own, (1 - side) * half, half, 0)
    came = mirror(send, ("yl",))
    image_x = jnp.where(side == 0, keep, came)
    modal_x = jnp.where(side == 0, came, keep)

    copies = jnp.broadcast_to(image_x[None], (16, half, width))
    copies, modal_x = stage(copies, modal_x)
    near = [jnp.concatenate([w0, modal_x])]
    near = [jnp.concatenate([near[0], pair(near[0], 0)])]
    far = [mirror(near[0], ("c",))]
    for step in (1, 2, 3):
        near.append(pair(near[-1], step))
        far.append(mirror(near[-1], ("c",)))
    image_x = lax.all_to_all(copies, PLANE, 0, 0)
    pieces = [image_x, *near, *far]

    table = pair_index.reshape(2, 8, 4, 2, 2, half)
    table = lax.dynamic_index_in_dim(table, z, 1, False)
    table = lax.dynamic_index_in_dim(table, core, 2, False)
    partner = table.transpose(2, 0, 1, 3).reshape(1, size)

    rows, flat = ((16, half, width), BF16), ((size, width), BF16)
    tile, one_line, square = ((8, size // 8), F32), ((1, size), F32), ((size, size), F32)
    some = ((2, 8, band, width), BF16)
    row_sum, col_sum, inv_img, inv_mod, x_mod, low_img, low_mod, res_img, res_mod, power, weight = call(
        score_kernel,
        at,
        scale,
        here_first(pieces, True),
        here_first([tile, tile, one_line, one_line], False) + here_first([rows, flat, flat, flat, flat, square, some], True),
        [rows, rows, some, some, flat, flat, flat, flat, square],
        4 * size * width * width + 2 * size * size * width,
    )
    def exchange(row_sum, col_sum, step):
        axes, mask = ((("x",), 1), (("x",), 3), (Y, 2), (Y, 3))[step]
        if step == 0:
            came = mirror(col_sum, ("c",))
        elif step == 3:
            came = across(col_sum)
        else:
            came = pair(col_sum, step)
        return stage(mirror(row_sum, axes, mask), came)

    for step in range(3):
        row_came, col_came = exchange(row_sum, col_sum, step)
        row_sum, col_sum = row_sum + row_came, col_sum + col_came
    row_came, col_came = exchange(row_sum, col_sum, 3)

    block = (8, 2 * band + half, width)
    d_image, keep, far, send = call(
        gradient_kernel,
        at,
        scale,
        here_first([row_sum, row_came, col_sum, col_came, partner, inv_img, inv_mod], False)
        + here_first([power, image_x, x_mod, low_img, low_mod, res_img, res_mod], True),
        here_first([rows, (block, BF16), ((2, *block[1:]), BF16), (block, BF16)], True),
        [square, rows, rows, flat, flat, flat, flat, ((size, size), BF16), rows, rows]
        + [(block, BF16), (block, BF16)],
        4 * size * width * width + 4 * size * size * width,
    )
    d_image = lax.all_to_all(d_image, PLANE, 0, 0)
    far, send = stage(mirror(far, ("c",)), send)
    mine = wider(keep[6:]) + wider(far)
    send = mirror(send, ("c",))
    for step, first in ((1, 4), (0, 2), (1, 0)):
        came = pair(mine.astype(BF16), step)
        if first == 0:
            came, d_image = stage(came, d_image)
        mine = wider(keep[first : first + 2]) + wider(send[first : first + 2]) + wider(came)
    sums = mine[0] + wider(pair(mine[1].astype(BF16), 0))
    d_image = jnp.sum(wider(d_image), axis=0)
    d_modal = sums[2 * band :]
    d_weight = sums[: 2 * band].reshape(16, band // 8, width)
    d_weight = jnp.sum(lax.all_to_all(d_weight, PLANE, 0, 0), axis=0, keepdims=True)

    came = mirror(jnp.where(side == 0, d_modal, d_image), ("yl",))
    d_proj = jnp.where(
        side == 0,
        jnp.concatenate([d_image, came]),
        jnp.concatenate([came, d_modal]),
    ).astype(BF16)
    d_inputs = lax.dot_general(
        d_proj, weight.reshape(width, width), (((1,), (1,)), ((), ())), preferred_element_type=F32
    )
    d_inputs = lax.dot_general(
        d_inputs.astype(BF16), reorder(width), (((1,), (1,)), ((), ())), preferred_element_type=F32
    )
    return (d_inputs.astype(BF16)[None], d_weight)


def solution(mesh):
    devices = mesh.devices.reshape([SIZES[name] for name in AXES])
    return jax.shard_map(
        per_device,
        mesh=Mesh(devices, AXES),
        in_specs=(P("yl", ROWS, None), P("yl", ROWS, None), P(), P()),
        out_specs=(P("yl", ROWS, None), P("yl", ROWS, None)),
        check_vma=False,
    )
```

```python
import jax
import jax.numpy as jnp
from jax import lax
from jax.experimental import pallas as pl
from jax.experimental.pallas import tpu as pltpu
from jax.sharding import Mesh, PartitionSpec as P

EPS = 1e-06
AXES = ("yl", "yh", "z", "x", "c")
SIZES = {"yl": 2, "yh": 2, "z": 8, "x": 4, "c": 2}
ROWS = ("yh", "z", "x", "c")
PLANE = ("yl", "yh", "x")
Y = ("yl", "yh")
F32 = jnp.float32
BF16 = jnp.bfloat16
LIMIT = 52 << 20
MEET = (0, 1, -1, -2, 2, 3, -3, -4)


def count(axes):
    total = 1
    for name in axes:
        total *= SIZES[name]
    return total


def mirror(value, axes, mask=1):
    return lax.ppermute(value, axes, [(i, i ^ mask) for i in range(count(axes))])


def pair(value, step):
    size = SIZES["z"]
    route = []
    for i in range(size):
        for core in range(2):
            kind = (core + step) % 2
            other = (((i + kind) ^ 1) - kind) % size
            route.append((2 * i + core, 2 * other + core))
    return lax.ppermute(value, ("z", "c"), route)


def across(value):
    size = SIZES["z"]
    route = []
    for i in range(size):
        for core in range(2):
            step = 3 if (i + core) % 2 else -3
            route.append((2 * i + core, 2 * ((i + step) % size) + core))
    return lax.ppermute(value, ("z", "c"), route)


def meets(z, core):
    sign = 1 - 2 * ((z + core) & 1)
    return [(z + sign * step) & 7 for step in MEET]


def gather(value, axes):
    copies = jnp.broadcast_to(value[None], (count(axes),) + value.shape)
    return lax.all_to_all(copies, axes, 0, 0)


def stage(*values):
    return lax.optimization_barrier(values)


def wider(value):
    return value.astype(F32)


def column(row):
    return jnp.transpose(jnp.broadcast_to(row, (128, row.shape[1])))[:, :1]


def line(values):
    return jnp.transpose(jnp.broadcast_to(values, (values.shape[0], 128)))[:1]


def mover(sems):
    used = []

    def move(source, target):
        copy = pltpu.make_async_copy(source, target, sems.at[len(used)])
        used.append(copy)
        copy.start()
        return copy

    return move


def arrive(copies):
    for copy in copies:
        copy.wait()


def fill(tile, values, first):
    for k in range(values.shape[1] // 128):
        tile[first + k : first + k + 1, :] = values[:, k * 128 : (k + 1) * 128]


def spread(tile):
    return jnp.concatenate([tile[k : k + 1, :] for k in range(tile.shape[0])], axis=1)


def score_kernel(at, scale, h_img, *refs):
    met = [refs[:4], refs[4:8]]
    (
        row_sum, col_sum, inv_img, inv_mod, o_mod, o_low_img, o_low_mod, o_res_img, o_res_mod, o_power,
        o_weight,
        x_img, x_mod, w_img, w_mod, low_img, low_mod, res_img, res_mod, power, sems,
    ) = refs[8:]
    core, z, side = at[0], at[1], at[4]
    half, width = x_img.shape[1], x_img.shape[2]
    band = w_img.shape[2]
    block = 2 * band + half
    size = 4 * half
    move = mover(sems)

    modal, image = [], []
    image.append(move(h_img, x_img))
    for want in (0, 1):
        for own in range(2):
            c = core if own == 0 else 1 - core
            for i, k in enumerate(meets(z, c)):
                piece, start = met[own][i // 2], (i % 2) * block
                if want == 0:
                    modal.append(move(piece.at[pl.ds(start + band, band)], w_mod.at[c, k]))
                    modal.append(move(piece.at[pl.ds(start + 2 * band, half)], x_mod.at[c * 8 + k]))
                else:
                    image.append(move(piece.at[pl.ds(start, band)], w_img.at[c, k]))

    going = []
    for rows, w, low, rest, inverse, to, needs in (
        (x_mod, w_mod, low_mod, res_mod, inv_mod, (o_low_mod, o_res_mod), modal),
        (x_img, w_img, low_img, res_img, inv_img, (o_low_img, o_res_img), image),
    ):
        arrive(needs)
        if rows is x_mod:
            going.append(move(x_mod, o_mod))
        for i in range(4):
            take = slice(i * size, (i + 1) * size)
            proj = jnp.dot(
                rows[4 * i : 4 * i + 4].reshape(size, width),
                w[...].reshape(width, width),
                preferred_element_type=F32,
            )
            inv = lax.rsqrt(jnp.sum(proj * proj, axis=1, keepdims=True) + EPS)
            proj = proj * inv
            head = proj.astype(BF16)
            low[take] = head
            rest[take] = (proj - wider(head)).astype(BF16)
            inverse[:, take] = line(inv)
        going += [move(low, to[0]), move(rest, to[1])]

    own = sems.at[sems.shape[0] - 1]

    @pl.when(side == 0)
    def _():
        pltpu.make_async_copy(w_img, o_weight, own).start()

    @pl.when(side == 1)
    def _():
        pltpu.make_async_copy(w_mod, o_weight, own).start()

    factor = scale[0]
    cols = None
    for i in range(4):
        take = slice(i * size, (i + 1) * size)
        scores = lax.dot_general(
            low_img[take], low_mod[...], (((1,), (1,)), ((), ())), preferred_element_type=F32
        )
        value = jnp.exp(factor * scores)
        power[take] = value
        going.append(move(power.at[take], o_power.at[take]))
        fill(row_sum, line(jnp.sum(value, axis=1, keepdims=True)), i * size // 128)
        part = jnp.sum(value, axis=0, keepdims=True)
        cols = part if cols is None else cols + part
    fill(col_sum, cols, 0)
    arrive(going)
    pltpu.make_async_copy(w_img, o_weight, own).wait()


def gradient_kernel(
    at, scale, row_sum, row_came, col_sum, col_came, partner, inv_img, inv_mod,
    h_power, h_img, h_mod, h_low_img, h_low_mod, h_res_img, h_res_mod,
    o_img, o_keep, o_far, o_send,
    power, x_img, x_mod, low_img, low_mod, res_img, res_mod,
    weight_row, p_img, p_mod, keep, send, sems,
):
    core, z, y, x, side = [at[i] for i in range(5)]
    half, width = x_img.shape[1], x_img.shape[2]
    wide, band = width // 2, width // 16
    size = 4 * half
    factor = scale[0]
    move = mover(sems)
    parts = [slice(i * size, (i + 1) * size) for i in range(4)]

    def load(i):
        pairs = ((h_power, power), (h_low_img, low_img), (h_res_img, res_img))
        return [move(source.at[parts[i]], target.at[parts[i]]) for source, target in pairs]

    first = move(h_power.at[parts[0]], power.at[parts[0]])
    low = move(h_low_mod, low_mod)
    needs = [
        move(h_low_img.at[parts[0]], low_img.at[parts[0]]),
        move(h_res_img.at[parts[0]], res_img.at[parts[0]]),
    ]
    loads = [load(1), load(2), load(3)]
    modal = [move(h_res_mod, res_mod)]
    rest = [move(h_img, x_img), move(h_mod, x_mod)]

    j = lax.broadcasted_iota(jnp.int32, (1, 16 * half), 1)
    jz, jc, jr = (j // half) & 7, j // (8 * half), j & (half - 1)
    ids = ((((y // 2) * 8 + jz) * 4 + x) * 2 + jc) * (2 * half) + side * half + jr
    col = 1.0 / spread(col_sum[...] + col_came[...])
    row = 1.0 / spread(row_sum[...] + row_came[...])

    def weigh(i):
        take = parts[i]
        hit = column(partner[:, take]) == ids
        value = power[take] * (column(row[:, take]) + col)
        weight_row[take] = (value - jnp.where(hit, 2.0, 0.0)).astype(BF16)

    def tangent(grad, low, rest, inv):
        unit = wider(low) + wider(rest)
        along = jnp.sum(grad * unit, axis=1, keepdims=True)
        return (column(factor * inv) * (grad - unit * along)).astype(BF16).reshape(4, half, width)

    arrive([first])
    weigh(0)
    arrive([low] + needs)
    for i, take in enumerate(parts):
        if i < 3:
            arrive(loads[i])
        grad = jnp.dot(weight_row[take], low_mod[...], preferred_element_type=F32)
        if i < 3:
            weigh(i + 1)
        p_img[4 * i : 4 * i + 4] = tangent(grad, low_img[take], res_img[take], inv_img[:, take])
    going = [move(p_img, o_img)]
    arrive(modal)
    for i, take in enumerate(parts):
        grad = lax.dot_general(
            weight_row[:, take], low_img[...], (((0,), (0,)), ((), ())), preferred_element_type=F32
        )
        p_mod[4 * i : 4 * i + 4] = tangent(grad, low_mod[take], res_mod[take], inv_mod[:, take])
    for c, target in ((core, keep), (1 - core, send)):
        for i, k in enumerate(meets(z, c)):
            target[i, 2 * band :] = p_mod[c * 8 + k]
    arrive(rest)
    for s, (rows, p) in enumerate(((x_img, p_img), (x_mod, p_mod))):
        lines = slice(s * band, (s + 1) * band)
        for c in range(2):
            grad = lax.dot_general(
                rows[:, :, c * wide : (c + 1) * wide].reshape(16 * half, wide),
                p[...].reshape(16 * half, width),
                (((0,), (0,)), ((), ())),
                preferred_element_type=F32,
            ).astype(BF16)
            sign = 1 - 2 * ((z + c) & 1)

            def put(target):
                for k in range(8):
                    step = (sign * (k - z)) & 7
                    spot = jnp.where(step < 2, step, jnp.where(step < 4, step + 2, 9 - step))
                    spot = jnp.where(step == 4, 7, jnp.where(step == 5, 6, spot))
                    target[spot, lines] = grad[k * band : (k + 1) * band]

            @pl.when(core == c)
            def _():
                put(keep)

            @pl.when(core != c)
            def _():
                put(send)

        for lines in (pl.ds(0, band), pl.ds(2 * band, half)) if s == 0 else (pl.ds(band, band),):
            for source, target in ((keep, o_keep), (send, o_send)):
                going.append(move(source.at[pl.ds(0, 8), lines], target.at[pl.ds(0, 8), lines]))
            going.append(move(send.at[pl.ds(6, 2), lines], o_far.at[pl.ds(0, 2), lines]))
    arrive(going)


def call(kernel, at, scale, operands, out, scratch, flops):
    spaces = {False: pl.BlockSpec(memory_space=pltpu.VMEM), True: pl.BlockSpec(memory_space=pl.ANY)}
    smem = pl.BlockSpec(memory_space=pltpu.SMEM)
    return pl.pallas_call(
        kernel,
        in_specs=[smem, smem] + [spaces[own] for _, own in operands],
        out_specs=[spaces[own] for _, own in out],
        out_shape=[jax.ShapeDtypeStruct(*one) for one, _ in out],
        scratch_shapes=[pltpu.VMEM(*one) for one in scratch] + [pltpu.SemaphoreType.DMA((96,))],
        compiler_params=pltpu.CompilerParams(vmem_limit_bytes=LIMIT),
        cost_estimate=pl.CostEstimate(flops=flops, bytes_accessed=8 << 20, transcendentals=0),
    )(at, scale, *[one for one, _ in operands])


def here_first(values, own):
    return [(one, own) for one in values]


def reorder(width):
    r = width // 128
    k = jnp.arange(width)
    low, c, x, z, yh = k % r, (k // r) % 2, (k // (2 * r)) % 4, (k // (8 * r)) % 8, k // (64 * r)
    to = (((c * 8 + z) * 2 + yh) * 4 + x) * r + low
    return (to[:, None] == k[None, :]).astype(BF16)


def per_device(embeds, weights, pair_index, scale):
    side = lax.axis_index("yl")
    yh, z, x, core = [lax.axis_index(name) for name in ROWS]
    at = jnp.stack([core, z, yh * 2 + side, x, side]).astype(jnp.int32)
    own, shard = embeds[0], weights[0]
    here, width = own.shape
    half, band, size = here // 2, 8 * shard.shape[0], 8 * here

    w0 = gather(shard, PLANE).reshape(2 * band, width)
    own = jnp.dot(own, reorder(width), preferred_element_type=F32).astype(BF16)

    keep = lax.dynamic_slice_in_dim(own, side * half, half, 0)
    send = lax.dynamic_slice_in_dim(own, (1 - side) * half, half, 0)
    came = mirror(send, ("yl",))
    image_x = jnp.where(side == 0, keep, came)
    modal_x = jnp.where(side == 0, came, keep)

    copies = jnp.broadcast_to(image_x[None], (16, half, width))
    copies, modal_x = stage(copies, modal_x)
    near = [jnp.concatenate([w0, modal_x])]
    near = [jnp.concatenate([near[0], pair(near[0], 0)])]
    far = [mirror(near[0], ("c",))]
    for step in (1, 2, 3):
        near.append(pair(near[-1], step))
        far.append(mirror(near[-1], ("c",)))
    image_x = lax.all_to_all(copies, PLANE, 0, 0)
    pieces = [image_x, *near, *far]

    table = pair_index.reshape(2, 8, 4, 2, 2, half)
    table = lax.dynamic_index_in_dim(table, z, 1, False)
    table = lax.dynamic_index_in_dim(table, core, 2, False)
    partner = table.transpose(2, 0, 1, 3).reshape(1, size)

    rows, flat = ((16, half, width), BF16), ((size, width), BF16)
    tile, one_line, square = ((8, size // 8), F32), ((1, size), F32), ((size, size), F32)
    some = ((2, 8, band, width), BF16)
    row_sum, col_sum, inv_img, inv_mod, x_mod, low_img, low_mod, res_img, res_mod, power, weight = call(
        score_kernel,
        at,
        scale,
        here_first(pieces, True),
        here_first([tile, tile, one_line, one_line], False) + here_first([rows, flat, flat, flat, flat, square, some], True),
        [rows, rows, some, some, flat, flat, flat, flat, square],
        4 * size * width * width + 2 * size * size * width,
    )
    def exchange(row_sum, col_sum, step):
        axes, mask = ((("x",), 1), (("x",), 3), (Y, 2), (Y, 3))[step]
        if step == 0:
            came = mirror(col_sum, ("c",))
        elif step == 3:
            came = across(col_sum)
        else:
            came = pair(col_sum, step)
        return stage(mirror(row_sum, axes, mask), came)

    for step in range(3):
        row_came, col_came = exchange(row_sum, col_sum, step)
        row_sum, col_sum = row_sum + row_came, col_sum + col_came
    row_came, col_came = exchange(row_sum, col_sum, 3)

    block = (8, 2 * band + half, width)
    d_image, keep, far, send = call(
        gradient_kernel,
        at,
        scale,
        here_first([row_sum, row_came, col_sum, col_came, partner, inv_img, inv_mod], False)
        + here_first([power, image_x, x_mod, low_img, low_mod, res_img, res_mod], True),
        here_first([rows, (block, BF16), ((2, *block[1:]), BF16), (block, BF16)], True),
        [square, rows, rows, flat, flat, flat, flat, ((size, size), BF16), rows, rows]
        + [(block, BF16), (block, BF16)],
        4 * size * width * width + 4 * size * size * width,
    )
    d_image = lax.all_to_all(d_image, PLANE, 0, 0)
    far, send = stage(mirror(far, ("c",)), send)
    mine = wider(keep[6:]) + wider(far)
    send = mirror(send, ("c",))
    for step, first in ((1, 4), (0, 2)):
        came = pair(mine.astype(BF16), step)
        mine = wider(keep[first : first + 2]) + wider(send[first : first + 2]) + wider(came)
    came, d_image = stage(pair(mine.astype(BF16), 1), d_image)
    mine = wider(keep[1]) + wider(send[1]) + wider(came[1])
    last, came = stage(pair(mine.astype(BF16), 0), came)
    sums = wider(keep[0]) + wider(send[0]) + wider(came[0]) + wider(last)
    d_image = jnp.sum(wider(d_image), axis=0)
    d_modal = sums[2 * band :]
    d_weight = sums[: 2 * band].reshape(16, band // 8, width)
    d_weight = jnp.sum(lax.all_to_all(d_weight, PLANE, 0, 0), axis=0, keepdims=True)

    came = mirror(jnp.where(side == 0, d_modal, d_image), ("yl",))
    d_proj = jnp.where(
        side == 0,
        jnp.concatenate([d_image, came]),
        jnp.concatenate([came, d_modal]),
    ).astype(BF16)
    d_inputs = lax.dot_general(
        d_proj, weight.reshape(width, width), (((1,), (1,)), ((), ())), preferred_element_type=F32
    )
    d_inputs = lax.dot_general(
        d_inputs.astype(BF16), reorder(width), (((1,), (1,)), ((), ())), preferred_element_type=F32
    )
    return (d_inputs.astype(BF16)[None], d_weight)


def solution(mesh):
    devices = mesh.devices.reshape([SIZES[name] for name in AXES])
    return jax.shard_map(
        per_device,
        mesh=Mesh(devices, AXES),
        in_specs=(P("yl", ROWS, None), P("yl", ROWS, None), P(), P()),
        out_specs=(P("yl", ROWS, None), P("yl", ROWS, None)),
        check_vma=False,
    )
```

```python
import jax
import jax.numpy as jnp
from jax import lax
from jax.experimental import pallas as pl
from jax.experimental.pallas import tpu as pltpu
from jax.sharding import Mesh, PartitionSpec as P

EPS = 1e-06
AXES = ("yl", "yh", "z", "x", "c")
SIZES = {"yl": 2, "yh": 2, "z": 8, "x": 4, "c": 2}
ROWS = ("yh", "z", "x", "c")
PLANE = ("yl", "yh", "x")
Y = ("yl", "yh")
F32 = jnp.float32
BF16 = jnp.bfloat16
LIMIT = 52 << 20
MEET = (0, 1, -1, -2, 2, 3, -3, -4)


def count(axes):
    total = 1
    for name in axes:
        total *= SIZES[name]
    return total


def mirror(value, axes, mask=1):
    return lax.ppermute(value, axes, [(i, i ^ mask) for i in range(count(axes))])


def pair(value, step):
    size = SIZES["z"]
    route = []
    for i in range(size):
        for core in range(2):
            kind = (core + step) % 2
            other = (((i + kind) ^ 1) - kind) % size
            route.append((2 * i + core, 2 * other + core))
    return lax.ppermute(value, ("z", "c"), route)


def across(value):
    size = SIZES["z"]
    route = []
    for i in range(size):
        for core in range(2):
            step = 3 if (i + core) % 2 else -3
            route.append((2 * i + core, 2 * ((i + step) % size) + core))
    return lax.ppermute(value, ("z", "c"), route)


def meets(z, core):
    sign = 1 - 2 * ((z + core) & 1)
    return [(z + sign * step) & 7 for step in MEET]


def gather(value, axes):
    copies = jnp.broadcast_to(value[None], (count(axes),) + value.shape)
    return lax.all_to_all(copies, axes, 0, 0)


def stage(*values):
    return lax.optimization_barrier(values)


def wider(value):
    return value.astype(F32)


def column(row):
    return jnp.transpose(jnp.broadcast_to(row, (128, row.shape[1])))[:, :1]


def line(values):
    return jnp.transpose(jnp.broadcast_to(values, (values.shape[0], 128)))[:1]


def mover(sems):
    used = []

    def move(source, target):
        copy = pltpu.make_async_copy(source, target, sems.at[len(used)])
        used.append(copy)
        copy.start()
        return copy

    return move


def arrive(copies):
    for copy in copies:
        copy.wait()


def fill(tile, values, first):
    for k in range(values.shape[1] // 128):
        tile[first + k : first + k + 1, :] = values[:, k * 128 : (k + 1) * 128]


def spread(tile):
    return jnp.concatenate([tile[k : k + 1, :] for k in range(tile.shape[0])], axis=1)


def score_kernel(at, scale, h_img, *refs):
    met = [refs[:4], refs[4:8]]
    (
        row_sum, col_sum, inv_img, inv_mod, o_mod, o_low_img, o_low_mod, o_res_img, o_res_mod, o_power,
        o_weight,
        x_img, x_mod, w_img, w_mod, low_img, low_mod, res_img, res_mod, power, sems,
    ) = refs[8:]
    core, z, side = at[0], at[1], at[4]
    half, width = x_img.shape[1], x_img.shape[2]
    band = w_img.shape[2]
    block = 2 * band + half
    size = 4 * half
    move = mover(sems)

    modal, image = [], []
    image.append(move(h_img, x_img))
    for want in (0, 1):
        for own in range(2):
            c = core if own == 0 else 1 - core
            for i, k in enumerate(meets(z, c)):
                piece, start = met[own][i // 2], (i % 2) * block
                if want == 0:
                    modal.append(move(piece.at[pl.ds(start + band, band)], w_mod.at[c, k]))
                    modal.append(move(piece.at[pl.ds(start + 2 * band, half)], x_mod.at[c * 8 + k]))
                else:
                    image.append(move(piece.at[pl.ds(start, band)], w_img.at[c, k]))

    going = []
    for rows, w, low, rest, inverse, to, needs in (
        (x_mod, w_mod, low_mod, res_mod, inv_mod, (o_low_mod, o_res_mod), modal),
        (x_img, w_img, low_img, res_img, inv_img, (o_low_img, o_res_img), image),
    ):
        arrive(needs)
        if rows is x_mod:
            going.append(move(x_mod, o_mod))
        for i in range(4):
            take = slice(i * size, (i + 1) * size)
            proj = jnp.dot(
                rows[4 * i : 4 * i + 4].reshape(size, width),
                w[...].reshape(width, width),
                preferred_element_type=F32,
            )
            inv = lax.rsqrt(jnp.sum(proj * proj, axis=1, keepdims=True) + EPS)
            proj = proj * inv
            head = proj.astype(BF16)
            low[take] = head
            rest[take] = (proj - wider(head)).astype(BF16)
            inverse[:, take] = line(inv)
        going += [move(low, to[0]), move(rest, to[1])]

    own = sems.at[sems.shape[0] - 1]

    @pl.when(side == 0)
    def _():
        pltpu.make_async_copy(w_img, o_weight, own).start()

    @pl.when(side == 1)
    def _():
        pltpu.make_async_copy(w_mod, o_weight, own).start()

    factor = scale[0]
    cols = None
    for i in range(4):
        take = slice(i * size, (i + 1) * size)
        scores = lax.dot_general(
            low_img[take], low_mod[...], (((1,), (1,)), ((), ())), preferred_element_type=F32
        )
        value = jnp.exp(factor * scores)
        power[take] = value
        going.append(move(power.at[take], o_power.at[take]))
        fill(row_sum, line(jnp.sum(value, axis=1, keepdims=True)), i * size // 128)
        part = jnp.sum(value, axis=0, keepdims=True)
        cols = part if cols is None else cols + part
    fill(col_sum, cols, 0)
    arrive(going)
    pltpu.make_async_copy(w_img, o_weight, own).wait()


def gradient_kernel(
    at, scale, row_sum, row_came, col_sum, col_came, partner, inv_img, inv_mod,
    h_power, h_img, h_mod, h_low_img, h_low_mod, h_res_img, h_res_mod,
    o_img, o_keep, o_far, o_send,
    power, x_img, x_mod, low_img, low_mod, res_img, res_mod,
    weight_row, p_img, p_mod, keep, send, sems,
):
    core, z, y, x, side = [at[i] for i in range(5)]
    half, width = x_img.shape[1], x_img.shape[2]
    wide, band = width // 2, width // 16
    size = 4 * half
    factor = scale[0]
    move = mover(sems)
    parts = [slice(i * size, (i + 1) * size) for i in range(4)]

    def load(i):
        pairs = ((h_power, power), (h_low_img, low_img), (h_res_img, res_img))
        return [move(source.at[parts[i]], target.at[parts[i]]) for source, target in pairs]

    first = move(h_power.at[parts[0]], power.at[parts[0]])
    low = move(h_low_mod, low_mod)
    needs = [
        move(h_low_img.at[parts[0]], low_img.at[parts[0]]),
        move(h_res_img.at[parts[0]], res_img.at[parts[0]]),
    ]
    loads = [load(1), load(2), load(3)]
    modal = [move(h_res_mod, res_mod)]
    rest = [move(h_img, x_img), move(h_mod, x_mod)]

    j = lax.broadcasted_iota(jnp.int32, (1, 16 * half), 1)
    jz, jc, jr = (j // half) & 7, j // (8 * half), j & (half - 1)
    ids = ((((y // 2) * 8 + jz) * 4 + x) * 2 + jc) * (2 * half) + side * half + jr
    col = 1.0 / spread(col_sum[...] + col_came[...])
    row = 1.0 / spread(row_sum[...] + row_came[...])

    def weigh(i):
        take = parts[i]
        hit = column(partner[:, take]) == ids
        value = power[take] * (column(row[:, take]) + col)
        weight_row[take] = (value - jnp.where(hit, 2.0, 0.0)).astype(BF16)

    def tangent(grad, low, rest, inv):
        unit = wider(low) + wider(rest)
        along = jnp.sum(grad * unit, axis=1, keepdims=True)
        return (column(factor * inv) * (grad - unit * along)).astype(BF16).reshape(4, half, width)

    arrive([first])
    weigh(0)
    arrive([low] + needs)
    for i, take in enumerate(parts):
        if i < 3:
            arrive(loads[i])
        grad = jnp.dot(weight_row[take], low_mod[...], preferred_element_type=F32)
        if i < 3:
            weigh(i + 1)
        p_img[4 * i : 4 * i + 4] = tangent(grad, low_img[take], res_img[take], inv_img[:, take])
    going = [move(p_img, o_img)]
    arrive(modal)
    for i, take in enumerate(parts):
        grad = lax.dot_general(
            weight_row[:, take], low_img[...], (((0,), (0,)), ((), ())), preferred_element_type=F32
        )
        p_mod[4 * i : 4 * i + 4] = tangent(grad, low_mod[take], res_mod[take], inv_mod[:, take])
    for c, target in ((core, keep), (1 - core, send)):
        for i, k in enumerate(meets(z, c)):
            target[i, 2 * band :] = p_mod[c * 8 + k]
    arrive(rest)
    for s, (rows, p) in enumerate(((x_img, p_img), (x_mod, p_mod))):
        lines = slice(s * band, (s + 1) * band)
        for c in range(2):
            grad = lax.dot_general(
                rows[:, :, c * wide : (c + 1) * wide].reshape(16 * half, wide),
                p[...].reshape(16 * half, width),
                (((0,), (0,)), ((), ())),
                preferred_element_type=F32,
            ).astype(BF16)
            sign = 1 - 2 * ((z + c) & 1)

            def put(target):
                for k in range(8):
                    step = (sign * (k - z)) & 7
                    spot = jnp.where(step < 2, step, jnp.where(step < 4, step + 2, 9 - step))
                    spot = jnp.where(step == 4, 7, jnp.where(step == 5, 6, spot))
                    target[spot, lines] = grad[k * band : (k + 1) * band]

            @pl.when(core == c)
            def _():
                put(keep)

            @pl.when(core != c)
            def _():
                put(send)

        for lines in (pl.ds(0, band), pl.ds(2 * band, half)) if s == 0 else (pl.ds(band, band),):
            for source, target in ((keep, o_keep), (send, o_send)):
                going.append(move(source.at[pl.ds(0, 8), lines], target.at[pl.ds(0, 8), lines]))
            going.append(move(send.at[pl.ds(6, 2), lines], o_far.at[pl.ds(0, 2), lines]))
    arrive(going)


def call(kernel, at, scale, operands, out, scratch, flops):
    spaces = {False: pl.BlockSpec(memory_space=pltpu.VMEM), True: pl.BlockSpec(memory_space=pl.ANY)}
    smem = pl.BlockSpec(memory_space=pltpu.SMEM)
    return pl.pallas_call(
        kernel,
        in_specs=[smem, smem] + [spaces[own] for _, own in operands],
        out_specs=[spaces[own] for _, own in out],
        out_shape=[jax.ShapeDtypeStruct(*one) for one, _ in out],
        scratch_shapes=[pltpu.VMEM(*one) for one in scratch] + [pltpu.SemaphoreType.DMA((96,))],
        compiler_params=pltpu.CompilerParams(vmem_limit_bytes=LIMIT),
        cost_estimate=pl.CostEstimate(flops=flops, bytes_accessed=8 << 20, transcendentals=0),
    )(at, scale, *[one for one, _ in operands])


def here_first(values, own):
    return [(one, own) for one in values]


def reorder(width):
    r = width // 128
    k = jnp.arange(width)
    low, c, x, z, yh = k % r, (k // r) % 2, (k // (2 * r)) % 4, (k // (8 * r)) % 8, k // (64 * r)
    to = (((c * 8 + z) * 2 + yh) * 4 + x) * r + low
    return (to[:, None] == k[None, :]).astype(BF16)


def per_device(embeds, weights, pair_index, scale):
    side = lax.axis_index("yl")
    yh, z, x, core = [lax.axis_index(name) for name in ROWS]
    at = jnp.stack([core, z, yh * 2 + side, x, side]).astype(jnp.int32)
    own, shard = embeds[0], weights[0]
    here, width = own.shape
    half, band, size = here // 2, 8 * shard.shape[0], 8 * here

    w0 = gather(shard, PLANE).reshape(2 * band, width)
    own = jnp.dot(own, reorder(width), preferred_element_type=F32).astype(BF16)

    keep = lax.dynamic_slice_in_dim(own, side * half, half, 0)
    send = lax.dynamic_slice_in_dim(own, (1 - side) * half, half, 0)
    came = mirror(send, ("yl",))
    image_x = jnp.where(side == 0, keep, came)
    modal_x = jnp.where(side == 0, came, keep)

    copies = jnp.broadcast_to(image_x[None], (16, half, width))
    copies, modal_x = stage(copies, modal_x)
    near = [jnp.concatenate([w0, modal_x])]
    near = [jnp.concatenate([near[0], pair(near[0], 0)])]
    far = [mirror(near[0], ("c",))]
    for step in (1, 2, 3):
        near.append(pair(near[-1], step))
        far.append(mirror(near[-1], ("c",)))
    image_x = lax.all_to_all(copies, PLANE, 0, 0)
    pieces = [image_x, *near, *far]

    table = pair_index.reshape(2, 8, 4, 2, 2, half)
    table = lax.dynamic_index_in_dim(table, z, 1, False)
    table = lax.dynamic_index_in_dim(table, core, 2, False)
    partner = table.transpose(2, 0, 1, 3).reshape(1, size)

    rows, flat = ((16, half, width), BF16), ((size, width), BF16)
    tile, one_line, square = ((8, size // 8), F32), ((1, size), F32), ((size, size), F32)
    some = ((2, 8, band, width), BF16)
    row_sum, col_sum, inv_img, inv_mod, x_mod, low_img, low_mod, res_img, res_mod, power, weight = call(
        score_kernel,
        at,
        scale,
        here_first(pieces, True),
        here_first([tile, tile, one_line, one_line], False) + here_first([rows, flat, flat, flat, flat, square, some], True),
        [rows, rows, some, some, flat, flat, flat, flat, square],
        4 * size * width * width + 2 * size * size * width,
    )
    def exchange(row_sum, col_sum, step):
        axes, mask = ((("x",), 1), (("x",), 3), (Y, 2), (Y, 3))[step]
        if step == 0:
            came = mirror(col_sum, ("c",))
        elif step == 3:
            came = across(col_sum)
        else:
            came = pair(col_sum, step)
        return mirror(row_sum, axes, mask), came

    for step in range(3):
        row_came, col_came = exchange(row_sum, col_sum, step)
        row_sum, col_sum = row_sum + row_came, col_sum + col_came
    row_came, col_came = exchange(row_sum, col_sum, 3)

    block = (8, 2 * band + half, width)
    d_image, keep, far, send = call(
        gradient_kernel,
        at,
        scale,
        here_first([row_sum, row_came, col_sum, col_came, partner, inv_img, inv_mod], False)
        + here_first([power, image_x, x_mod, low_img, low_mod, res_img, res_mod], True),
        here_first([rows, (block, BF16), ((2, *block[1:]), BF16), (block, BF16)], True),
        [square, rows, rows, flat, flat, flat, flat, ((size, size), BF16), rows, rows]
        + [(block, BF16), (block, BF16)],
        4 * size * width * width + 4 * size * size * width,
    )
    d_image = lax.all_to_all(d_image, PLANE, 0, 0)
    far, send = stage(mirror(far, ("c",)), send)
    mine = wider(keep[6:]) + wider(far)
    send = mirror(send, ("c",))
    for step, first in ((1, 4), (0, 2), (1, 0)):
        came = pair(mine.astype(BF16), step)
        if first == 0:
            came, d_image = stage(came, d_image)
        mine = wider(keep[first : first + 2]) + wider(send[first : first + 2]) + wider(came)
    sums = mine[0] + wider(pair(mine[1].astype(BF16), 0))
    d_image = jnp.sum(wider(d_image), axis=0)
    d_modal = sums[2 * band :]
    d_weight = sums[: 2 * band].reshape(16, band // 8, width)
    d_weight = jnp.sum(lax.all_to_all(d_weight, PLANE, 0, 0), axis=0, keepdims=True)

    came = mirror(jnp.where(side == 0, d_modal, d_image), ("yl",))
    d_proj = jnp.where(
        side == 0,
        jnp.concatenate([d_image, came]),
        jnp.concatenate([came, d_modal]),
    ).astype(BF16)
    d_inputs = lax.dot_general(
        d_proj, weight.reshape(width, width), (((1,), (1,)), ((), ())), preferred_element_type=F32
    )
    d_inputs = lax.dot_general(
        d_inputs.astype(BF16), reorder(width), (((1,), (1,)), ((), ())), preferred_element_type=F32
    )
    return (d_inputs.astype(BF16)[None], d_weight)


def solution(mesh):
    devices = mesh.devices.reshape([SIZES[name] for name in AXES])
    return jax.shard_map(
        per_device,
        mesh=Mesh(devices, AXES),
        in_specs=(P("yl", ROWS, None), P("yl", ROWS, None), P(), P()),
        out_specs=(P("yl", ROWS, None), P("yl", ROWS, None)),
        check_vma=False,
    )
```
